256 devices in a mesh: wide: 64 (over x, z, core), narrow: 4 (over y).
Axes of the slice: x: 4, y: 4, z: 8, core: 2. Of those that a mesh axis runs over, the one named last changes fastest.
Arguments:
- potentials: float32 [64, 128, 128, 128], P('wide', 'narrow'), may hold values from -190 to 190
- parents: int32 [64], replicated, may hold values from 0 to 20, as said below
- separator_excluded: int32 [64], replicated, may hold values from 0 to 2
- measurement_clique: int32 [64], replicated, may hold values from 0 to 63, as said below
- measured: float32 [64, 128, 128], P('wide', 'narrow'), may hold values from 0.25 to 4
Outputs:
- marginal: float32 [64, 128, 128], P('wide', 'narrow')
- updated: float32 [64, 128, 128, 128], P('wide', 'narrow')
The draws below stay inside these ranges and needn't reach their ends.
Inputs may be any that keep to these rules, and one draw needn't show every extreme that they name: parents[0] = 0; a clique c with 1 <= c < 5 has parent 0, one with 5 <= c < 21 a parent in 1 to 4, and one with c >= 21 a parent in 5 to 20; the last clique has parent 21 - 1. `measurement_clique`: every clique is named by exactly one measured marginal.
All inputs are finite; a program needn't handle non-finite values.
Results may differ from the reference program's by a relative error of at most 0.0003.
Values sent between devices are 32-bit elements; how exact they have to be, the bound alone decides.
A program may use at most 64 MiB of HBM per device.

```python
import math
import jax
import jax.numpy as jnp
from jax import lax

K = 128
DEPTH = 3
CLIQUE_COUNT = 64
LEVEL1 = 5
LEVEL2 = 21


def draw_parents(key, part):
    clique_numbers = jnp.arange(CLIQUE_COUNT, dtype=jnp.int32)
    lowest = jnp.where(clique_numbers < LEVEL1, 0, jnp.where(clique_numbers < LEVEL2, 1, LEVEL1)).astype(jnp.int32)
    beyond = jnp.where(clique_numbers < LEVEL1, 1, jnp.where(clique_numbers < LEVEL2, LEVEL1, LEVEL2)).astype(jnp.int32)
    raw_draw = jax.random.randint(key, (CLIQUE_COUNT,), 0, 1 << 20, dtype=jnp.int32)
    picked = (lowest + raw_draw % (beyond - lowest)).astype(jnp.int32)
    return jnp.where(clique_numbers == CLIQUE_COUNT - 1, LEVEL2 - 1, picked).astype(jnp.int32)


def draw_measurement_clique(key, part):
    count = CLIQUE_COUNT
    numbers = jnp.arange(count, dtype=jnp.int32)
    fixed_sources = jnp.array([count - 2, LEVEL2 + 1, (LEVEL2 + 1 + count // 2) % count], jnp.int32)
    fixed_targets = jnp.array([count - 1, LEVEL2, LEVEL2 + 1], jnp.int32)
    source_fixed = jnp.any(numbers[:, None] == fixed_sources[None, :], axis=1)
    target_fixed = jnp.any(numbers[:, None] == fixed_targets[None, :], axis=1)
    source_order = jnp.argsort(source_fixed.astype(jnp.int32) * count + numbers, stable=True).astype(jnp.int32)
    scores = jax.random.permutation(jax.random.fold_in(key, 11), count).astype(jnp.int32)
    target_order = jnp.argsort(target_fixed.astype(jnp.int32) * count + scores, stable=True).astype(jnp.int32)
    result = jnp.zeros((count,), jnp.int32).at[source_order].set(target_order)
    result = result.at[fixed_sources].set(fixed_targets)
    return result.astype(jnp.int32)


def draw_potentials(key, part):
    noise = jax.random.normal(key, (CLIQUE_COUNT, K, K, K), jnp.float32) * 1.5
    return jnp.clip(noise, -9.0, 9.0)


def with_ends(entries, rng, smallest, largest):
    place = [jax.random.randint(jax.random.fold_in(rng, axis), (), 0, length) for axis, length in enumerate(entries.shape)]
    longest = entries.shape.index(max(entries.shape))
    neighbour = place[:longest] + [(place[longest] + 1) % entries.shape[longest]] + place[longest + 1:]
    return entries.at[tuple(place)].set(smallest).at[tuple(neighbour)].set(largest)


def steps_of(stream_key, shape, shards, smallest, high):
    def one(axis_at, shards_of):
        steps = jax.random.uniform(jax.random.fold_in(jax.random.fold_in(stream_key, 6), axis_at), (shards_of,), jnp.float32, smallest / len(shards), high / len(shards))
        return jnp.repeat(jnp.exp(steps), shape[axis_at] // shards_of).reshape((-1,) + (1,) * (len(shape) - axis_at - 1))

    level = one(*shards[0])
    for cut in shards[1:]:
        level = level * one(*cut)
    return level


def setup_inputs(seed: int = 0) -> dict:
    streams_of = jax.random.split(jax.random.key(seed), 6)
    return {
        "potentials": draw_potentials(jax.random.fold_in(streams_of[5], 71), 0),
        "parents": draw_parents(jax.random.fold_in(streams_of[5], 71), 0),
        "separator_excluded": with_ends(jax.random.randint(streams_of[2], (CLIQUE_COUNT,), 0, 3), jax.random.fold_in(streams_of[2], 1), 0, 2).astype(jnp.int32),
        "measurement_clique": draw_measurement_clique(jax.random.fold_in(streams_of[5], 71), 0),
        "measured": jnp.clip(jnp.exp(math.log(4.0) - 2.7725887 * jax.random.uniform(streams_of[4], (CLIQUE_COUNT, K, K), jnp.float32) ** steps_of(streams_of[4], (CLIQUE_COUNT, K, K), ((0, 64), (1, 4)), -0.2, 0.2)), 0.25, 4.0),
    }


def log_sum(values, along):
    largest_entry = jnp.max(values, axis=along, keepdims=True)
    return jnp.squeeze(largest_entry, along) + jnp.log(jnp.sum(jnp.exp(values - largest_entry), axis=along))


def three_ways(table):
    return jnp.stack([log_sum(table, 0), log_sum(table, 1), log_sum(table, 2)])


def first_way(table):
    return log_sum(table, 0)


def reference(potentials, parents, separator_excluded, measurement_clique, measured):
    clique_numbers = jnp.arange(CLIQUE_COUNT, dtype=jnp.int32)
    belief = potentials
    for iteration in range(DEPTH):
        messages = lax.map(three_ways, belief)
        incoming = messages[parents, separator_excluded]
        incoming = jnp.where((clique_numbers > 0)[:, None, None], incoming, jnp.float32(0.0))
        belief = potentials + incoming[:, None, :, :]
    cell_lse = lax.map(first_way, belief)
    logz = log_sum(cell_lse.reshape(CLIQUE_COUNT, K * K), 1)
    marginal = jnp.float32(K * K) * jnp.exp(cell_lse - logz[:, None, None])
    sender_rows = jnp.zeros((CLIQUE_COUNT,), jnp.int32).at[measurement_clique].set(clique_numbers)
    residual = marginal - measured[sender_rows]
    is_leaf = (clique_numbers >= LEVEL2)[:, None, None]
    step_term = jnp.where(is_leaf, residual, jnp.float32(0.0))
    updated = potentials - jnp.float32(0.5) * step_term[:, None, :, :]
    return marginal, updated
```

```python
import jax
import jax.numpy as jnp
from jax import lax
from jax.experimental import pallas as pl
from jax.experimental.pallas import tpu as pltpu
from jax.sharding import PartitionSpec as P

MESH = pl.DeviceIdType.MESH
K = 128
QUARTERS = 4
ROWS = K // QUARTERS
CLIQUES = 64
LEVEL1, LEVEL2 = 5, 21
FIRST = LEVEL1 - 1
SECOND = LEVEL2 - LEVEL1
LEAVES = CLIQUES - LEVEL2
SUB = ROWS // SECOND


def sweep_kernel(
    parents, kinds, targets, pot, measured, out,
    partial, partial_in, own_l0, message, message_t, pot_t, top, total, tables,
    to_first, to_second, candidates, sub_tables, relay_tables,
    sub_measured, relay_measured, to_leaf, from_relay, final,
    sem_l0, sem_first, sem_second, sem_rows, sem_relay, sem_measured, sem_leaf, sem_final,
):
    me = lax.axis_index("wide")
    quarter = lax.axis_index("narrow")
    is_root = me == 0
    is_first = jnp.logical_and(me >= 1, me < LEVEL1)
    is_second = jnp.logical_and(me >= LEVEL1, me < LEVEL2)
    is_leaf = me >= LEVEL2
    is_inner = me < LEVEL2

    def peer(step):
        return lax.rem(quarter + step, QUARTERS)

    def repeat(count, function):
        def run(index, carry):
            function(index)
            return carry

        lax.fori_loop(0, count, run, 0)

    def send(source, target, sem, device):
        pltpu.make_async_remote_copy(
            src_ref=source, dst_ref=target, send_sem=sem.at[0], recv_sem=sem.at[1],
            device_id=device, device_id_type=MESH,
        ).start()

    def await_bytes(like, sem, which):
        pltpu.make_async_copy(like, like, sem.at[which]).wait()

    barrier = pltpu.get_barrier_semaphore()

    def greet(wide, narrow):
        pl.semaphore_signal(barrier, inc=1, device_id=(wide, narrow), device_id_type=MESH)

    for step in range(1, QUARTERS):
        greet(me, peer(step))

    @pl.when(is_first)
    def _():
        for other in range(QUARTERS):
            greet(0, other)

    @pl.when(is_second)
    def _():
        def one(step):
            greet(lax.rem(me + 1 + step, CLIQUES), quarter)

        repeat(CLIQUES - 1, one)

    @pl.when(is_leaf)
    def _():
        repeat(SECOND, lambda relay: greet(LEVEL1 + relay, quarter))

    for relay in range(SECOND):
        sub_measured[relay] = measured[relay * SUB:(relay + 1) * SUB, :]

    def partial_lse(block):
        rows = pl.ds(pl.multiple_of(block * 8, 8), 8)
        slab = pot[:, rows, :]
        largest = jnp.max(slab, axis=0)
        partial[rows, :] = largest + jnp.log(jnp.sum(jnp.exp(slab - largest[None]), axis=0))

    repeat(K // 8, partial_lse)

    peers = QUARTERS - 1

    @pl.when(is_root)
    def _():
        pl.semaphore_wait(barrier, peers + SECOND + FIRST * QUARTERS)

    @pl.when(jnp.logical_or(is_first, is_leaf))
    def _():
        pl.semaphore_wait(barrier, peers + SECOND)

    @pl.when(is_second)
    def _():
        pl.semaphore_wait(barrier, peers + SECOND - 1 + LEAVES)

    for step in range(1, QUARTERS):
        rows = pl.ds(pl.multiple_of(peer(step) * ROWS, ROWS), ROWS)
        send(partial.at[rows], partial_in.at[step - 1], sem_l0, (me, peer(step)))

    def give_measured(relay):
        @pl.when(me != LEVEL1 + relay)
        def _():
            send(sub_measured.at[relay], relay_measured.at[me], sem_measured, (LEVEL1 + relay, quarter))

    repeat(SECOND, give_measured)

    @pl.when(is_inner)
    def _():
        def turn(a0):
            pot_t[a0] = pot[a0].T

        repeat(ROWS, turn)

    @pl.when(is_root)
    def _():
        message[...] = jnp.zeros_like(message)

    @pl.when(is_first)
    def _():
        await_bytes(message, sem_first, 1)

    @pl.when(is_second)
    def _():
        await_bytes(candidates, sem_second, 1)
        message[quarter] = candidates[jnp.maximum(parents[me] - 1, 0)]
        for step in range(1, QUARTERS):
            send(message.at[quarter], message.at[quarter], sem_rows, (me, peer(step)))
        await_bytes(message.at[pl.ds(0, QUARTERS - 1)], sem_rows, 1)

    @pl.when(is_inner)
    def _():
        for other in range(QUARTERS):
            message_t[:, other * ROWS:(other + 1) * ROWS] = message[other].T

        def reduce_rows(a0):
            row = pl.ds(a0, 1)
            for kind in (1, 2):
                if kind == 1:
                    belief = pot[a0].reshape(QUARTERS, ROWS, K) + message[...]
                    belief = belief.reshape(K, K)
                else:
                    belief = pot_t[a0] + message_t[...]
                largest = jnp.max(belief, axis=0, keepdims=True)
                top[kind - 1, row, :] = largest
                total[kind - 1, row, :] = jnp.sum(jnp.exp(belief - largest), axis=0, keepdims=True)

        repeat(ROWS, reduce_rows)
        for kind in (1, 2):
            tables[kind] = top[kind - 1] + jnp.log(total[kind - 1])

    await_bytes(partial_in, sem_l0, 1)
    mine = partial[pl.ds(pl.multiple_of(quarter * ROWS, ROWS), ROWS), :]
    largest = jnp.maximum(mine, jnp.max(partial_in[...], axis=0))
    summed = jnp.exp(mine - largest) + jnp.sum(jnp.exp(partial_in[...] - largest[None]), axis=0)
    own_l0[...] = largest + jnp.log(summed)

    @pl.when(is_inner)
    def _():
        tables[0] = own_l0[...] + message[quarter]
        final[0] = tables[0]
        final[1] = jnp.zeros_like(final[1])

    @pl.when(is_root)
    def _():
        for child in range(FIRST):
            to_first[child] = tables[kinds[1 + child]]
            for other in range(QUARTERS):
                send(to_first.at[child], message.at[quarter], sem_first, (1 + child, other))

    @pl.when(is_first)
    def _():
        def give(child):
            to_second[child] = tables[kinds[LEVEL1 + child]]
            send(to_second.at[child], candidates.at[me - 1], sem_second, (LEVEL1 + child, quarter))

        repeat(SECOND, give)

    @pl.when(is_second)
    def _():
        slot = me - LEVEL1
        for kind in range(3):
            for relay in range(SECOND):
                sub_tables[relay, kind] = tables[kind, relay * SUB:(relay + 1) * SUB, :]

        def give_tables(relay):
            @pl.when(slot != relay)
            def _():
                send(sub_tables.at[relay], relay_tables.at[slot], sem_relay, (LEVEL1 + relay, quarter))

        repeat(SECOND, give_tables)
        relay_tables[slot] = sub_tables[slot]
        await_bytes(relay_measured.at[pl.ds(0, CLIQUES - 1)], sem_measured, 1)
        relay_measured[me] = sub_measured[slot]
        clique = lax.broadcasted_iota(jnp.int32, (CLIQUES, CLIQUES), 0)
        chosen = (clique == targets[...]).astype(jnp.float32)
        for row in range(SUB):
            to_leaf[:, 1, row, :] = jnp.dot(
                chosen, relay_measured[:, row, :],
                precision=lax.Precision.HIGHEST, preferred_element_type=jnp.float32,
            )
        await_bytes(relay_tables.at[pl.ds(0, SECOND - 1)], sem_relay, 1)

        def give_leaf(leaf):
            child = LEVEL2 + leaf
            to_leaf[child, 0] = relay_tables[jnp.maximum(parents[child] - LEVEL1, 0), kinds[child]]
            send(to_leaf.at[child], from_relay.at[slot], sem_leaf, (child, quarter))

        repeat(LEAVES, give_leaf)

    @pl.when(is_leaf)
    def _():
        await_bytes(from_relay, sem_leaf, 1)
        for relay in range(SECOND):
            rows = slice(relay * SUB, (relay + 1) * SUB)
            final[0, rows, :] = own_l0[rows, :] + from_relay[relay, 0]
            final[1, rows, :] = from_relay[relay, 1]

    for step in range(1, QUARTERS):
        send(final, out.at[quarter], sem_final, (me, peer(step)))
    out[quarter] = final[...]
    await_bytes(out.at[pl.ds(0, QUARTERS - 1)], sem_final, 1)

    await_bytes(partial_in, sem_l0, 0)
    await_bytes(out.at[pl.ds(0, QUARTERS - 1)], sem_final, 0)

    @pl.when(is_root)
    def _():
        for _ in range(QUARTERS):
            await_bytes(to_first, sem_first, 0)

    @pl.when(is_first)
    def _():
        await_bytes(to_second, sem_second, 0)

    @pl.when(is_second)
    def _():
        await_bytes(message.at[pl.ds(0, QUARTERS - 1)], sem_rows, 0)
        await_bytes(relay_tables.at[pl.ds(0, SECOND - 1)], sem_relay, 0)
        await_bytes(relay_measured.at[pl.ds(0, SECOND - 1)], sem_measured, 0)
        await_bytes(to_leaf.at[pl.ds(0, LEAVES)], sem_leaf, 0)

    @pl.when(jnp.logical_not(is_second))
    def _():
        await_bytes(sub_measured, sem_measured, 0)


def sweep(parents, kinds, targets, pot, measured):
    vmem, smem = pl.BlockSpec(memory_space=pltpu.VMEM), pl.BlockSpec(memory_space=pltpu.SMEM)
    f32 = jnp.float32
    scratch = [
        (K, K), (QUARTERS - 1, ROWS, K), (ROWS, K), (QUARTERS, ROWS, K), (K, K), (ROWS, K, K),
        (2, ROWS, K), (2, ROWS, K), (3, ROWS, K),
        (FIRST, ROWS, K), (SECOND, ROWS, K), (FIRST, ROWS, K), (SECOND, 3, SUB, K), (SECOND, 3, SUB, K),
        (SECOND, SUB, K), (CLIQUES, SUB, K), (CLIQUES, 2, SUB, K), (SECOND, 2, SUB, K), (2, ROWS, K),
    ]
    return pl.pallas_call(
        sweep_kernel,
        out_shape=jax.ShapeDtypeStruct((QUARTERS, 2, ROWS, K), f32),
        in_specs=[smem, smem, vmem, vmem, vmem],
        out_specs=vmem,
        scratch_shapes=[pltpu.VMEM(shape, f32) for shape in scratch] + [pltpu.SemaphoreType.DMA((2,))] * 8,
        compiler_params=pltpu.CompilerParams(
            collective_id=0, has_side_effects=True, vmem_limit_bytes=24 * 1024 * 1024
        ),
        name="sweep",
    )(parents, kinds, targets, pot, measured)


BLOCK = 8


def finish_kernel(final, pot, marginal, updated, term):
    me = lax.axis_index("wide")
    quarter = lax.axis_index("narrow")

    @pl.when(pl.program_id(0) == 0)
    def _():
        cells = final[:, 0]
        largest = jnp.max(cells)
        weights = jnp.exp(cells - largest)
        scale = jnp.float32(K * K) / jnp.sum(weights)
        whole = weights * scale
        residual = whole - final[:, 1]
        term[...] = jnp.where(me >= LEVEL2, jnp.float32(0.5) * residual, jnp.float32(0.0))
        own = final[quarter, 0]
        marginal[...] = jnp.exp(own - largest) * scale

    for other in range(QUARTERS):
        rows = slice(other * ROWS, (other + 1) * ROWS)
        updated[:, rows, :] = pot[:, rows, :] - term[other][None]


def finish(final, pot):
    return pl.pallas_call(
        finish_kernel,
        grid=(ROWS // BLOCK,),
        out_shape=(
            jax.ShapeDtypeStruct((ROWS, K), jnp.float32),
            jax.ShapeDtypeStruct((ROWS, K, K), jnp.float32),
        ),
        in_specs=[
            pl.BlockSpec((QUARTERS, 2, ROWS, K), lambda i: (0, 0, 0, 0)),
            pl.BlockSpec((BLOCK, K, K), lambda i: (i, 0, 0)),
        ],
        out_specs=(
            pl.BlockSpec((ROWS, K), lambda i: (0, 0)),
            pl.BlockSpec((BLOCK, K, K), lambda i: (i, 0, 0)),
        ),
        scratch_shapes=[pltpu.VMEM((QUARTERS, ROWS, K), jnp.float32)],
        name="finish",
    )(final, pot)


def body(potentials, parents, separator_excluded, measurement_clique, measured):
    pot = potentials[0]
    final = sweep(parents, separator_excluded, measurement_clique[None], pot, measured[0])
    marginal, updated = finish(final, pot)
    return marginal[None], updated[None]


def solution(mesh):
    return jax.shard_map(
        body,
        mesh=mesh,
        in_specs=(P("wide", "narrow", None, None), P(), P(), P(), P("wide", "narrow", None)),
        out_specs=(P("wide", "narrow", None), P("wide", "narrow", None, None)),
        check_vma=False,
    )
```

```python
import jax
import jax.numpy as jnp
from jax import lax
from jax.experimental import pallas as pl
from jax.experimental.pallas import tpu as pltpu
from jax.sharding import PartitionSpec as P

MESH = pl.DeviceIdType.MESH
K = 128
QUARTERS = 4
ROWS = K // QUARTERS
CLIQUES = 64
LEVEL1, LEVEL2 = 5, 21
FIRST = LEVEL1 - 1
SECOND = LEVEL2 - LEVEL1
LEAVES = CLIQUES - LEVEL2
SUB = ROWS // SECOND


def sweep_kernel(
    parents_hbm, kinds_hbm, targets_hbm, pot_hbm, measured_hbm, out, pot,
    parents, kinds, targets, measured,
    partial, partial_in, own_l0, whole_l0, message, message_t, pot_t, tables,
    to_first, to_second, candidates, sub_tables, relay_tables,
    sub_measured, forwarded, relay_measured, to_leaf, from_relay,
    sem_small, sem_pot,
    sem_l0, sem_whole, sem_first, sem_second, sem_rows, sem_relay, sem_forward, sem_measured, sem_leaf,
):
    me = lax.axis_index("wide")
    quarter = lax.axis_index("narrow")
    is_root = me == 0
    is_first = jnp.logical_and(me >= 1, me < LEVEL1)
    is_second = jnp.logical_and(me >= LEVEL1, me < LEVEL2)
    is_leaf = me >= LEVEL2
    is_inner = me < LEVEL2
    peers = QUARTERS - 1

    def peer(step):
        return lax.rem(quarter + step, QUARTERS)

    def rows_of(part):
        return pl.ds(pl.multiple_of(part * ROWS, ROWS), ROWS)

    def repeat(count, function, unroll=1):
        def run(index, carry):
            function(index)
            return carry

        lax.fori_loop(0, count, run, 0, unroll=unroll)

    def send(source, target, sem, device):
        pltpu.make_async_remote_copy(
            src_ref=source, dst_ref=target, send_sem=sem.at[0], recv_sem=sem.at[1],
            device_id=device, device_id_type=MESH,
        ).start()

    def await_bytes(like, sem, which):
        pltpu.make_async_copy(like, like, sem.at[which]).wait()

    small = [
        pltpu.make_async_copy(source, target, sem_small.at[index])
        for index, (source, target) in enumerate(
            ((parents_hbm, parents), (kinds_hbm, kinds), (targets_hbm, targets), (measured_hbm, measured))
        )
    ]

    def pot_copy(step):
        rows = rows_of(peer(step))
        return pltpu.make_async_copy(pot_hbm.at[:, rows], pot.at[:, rows], sem_pot.at[step])

    order = (1, 2, 3, 0)
    for step in order:
        pot_copy(step).start()
    for copy in small:
        copy.start()

    barrier = pltpu.get_barrier_semaphore()

    def greet(wide, narrow):
        pl.semaphore_signal(barrier, inc=1, device_id=(wide, narrow), device_id_type=MESH)

    for step in range(1, QUARTERS):
        greet(me, peer(step))

    @pl.when(is_first)
    def _():
        greet(0, quarter)

    @pl.when(is_second)
    def _():
        def one(index):
            greet(1 + index + (index >= me - 1).astype(jnp.int32), quarter)

        repeat(CLIQUES - 2, one)

    @pl.when(is_leaf)
    def _():
        def one(index):
            greet(LEVEL1 + index // QUARTERS, lax.rem(index, QUARTERS))

        repeat(SECOND * QUARTERS, one)

    def partial_lse(step):
        base = peer(step) * ROWS

        def one(block):
            rows = pl.ds(pl.multiple_of(base + block * 8, 8), 8)
            slab = pot[:, rows, :]
            largest = jnp.max(slab, axis=0)
            partial[rows, :] = largest + jnp.log(jnp.sum(jnp.exp(slab - largest[None]), axis=0))

        pot_copy(step).wait()
        repeat(ROWS // 8, one, unroll=2)

    partial_lse(1)

    @pl.when(is_root)
    def _():
        pl.semaphore_wait(barrier, peers + FIRST)

    @pl.when(is_first)
    def _():
        pl.semaphore_wait(barrier, peers + SECOND)

    @pl.when(is_leaf)
    def _():
        pl.semaphore_wait(barrier, peers + SECOND)

    @pl.when(is_second)
    def _():
        pl.semaphore_wait(barrier, peers + SECOND - 1 + LEAVES * QUARTERS)

    for step in order:
        if step != order[0]:
            partial_lse(step)
        if step:
            send(partial.at[rows_of(peer(step))], partial_in.at[step - 1], sem_l0, (me, peer(step)))

    for copy in small:
        copy.wait()
    for relay in range(SECOND):
        sub_measured[relay] = measured[relay * SUB:(relay + 1) * SUB, :]

    @pl.when(is_root)
    def _():
        send(sub_measured, forwarded, sem_forward, (1, quarter))

    @pl.when(jnp.logical_not(is_root))
    def _():
        def give(relay):
            @pl.when(me != LEVEL1 + relay)
            def _():
                send(sub_measured.at[relay], relay_measured.at[me], sem_measured, (LEVEL1 + relay, quarter))

        repeat(SECOND, give)

    @pl.when(me == 1)
    def _():
        await_bytes(forwarded, sem_forward, 1)

        def give(relay):
            send(forwarded.at[relay], relay_measured.at[0], sem_measured, (LEVEL1 + relay, quarter))

        repeat(SECOND, give)

    @pl.when(is_inner)
    def _():
        def turn(a0):
            pot_t[a0] = pot[a0].T

        repeat(ROWS, turn, unroll=4)

    @pl.when(is_root)
    def _():
        message[...] = jnp.zeros_like(message)

    @pl.when(is_first)
    def _():
        await_bytes(message, sem_first, 1)

    @pl.when(is_second)
    def _():
        await_bytes(candidates, sem_second, 1)
        message[quarter] = candidates[jnp.maximum(parents[me] - 1, 0)]
        for step in range(1, QUARTERS):
            send(message.at[quarter], message.at[quarter], sem_rows, (me, peer(step)))
        await_bytes(message.at[pl.ds(0, QUARTERS - 1)], sem_rows, 1)

    @pl.when(is_inner)
    def _():
        for other in range(QUARTERS):
            message_t[:, other * ROWS:(other + 1) * ROWS] = message[other].T

        def eight(group):
            rows = pl.ds(pl.multiple_of(group * 8, 8), 8)
            for kind in (1, 2):
                tops, totals = [], []
                for step in range(8):
                    a0 = group * 8 + step
                    if kind == 1:
                        belief = (pot[a0].reshape(QUARTERS, ROWS, K) + message[...]).reshape(K, K)
                    else:
                        belief = pot_t[a0] + message_t[...]
                    largest = jnp.max(belief, axis=0, keepdims=True)
                    tops.append(largest)
                    totals.append(jnp.sum(jnp.exp(belief - largest), axis=0, keepdims=True))
                tables[kind, rows, :] = jnp.concatenate(tops, 0) + jnp.log(jnp.concatenate(totals, 0))

        repeat(ROWS // 8, eight)

    await_bytes(partial_in, sem_l0, 1)
    mine = partial[rows_of(quarter), :]
    largest = jnp.maximum(mine, jnp.max(partial_in[...], axis=0))
    summed = jnp.exp(mine - largest) + jnp.sum(jnp.exp(partial_in[...] - largest[None]), axis=0)
    own_l0[...] = largest + jnp.log(summed)

    @pl.when(is_inner)
    def _():
        tables[0] = own_l0[...] + message[quarter]

    @pl.when(is_root)
    def _():
        for child in range(FIRST):
            to_first[child] = tables[kinds[1 + child]]
            for other in range(QUARTERS):
                send(to_first.at[child], message.at[quarter], sem_first, (1 + child, other))

    @pl.when(is_first)
    def _():
        def give(child):
            to_second[child] = tables[kinds[LEVEL1 + child]]
            send(to_second.at[child], candidates.at[me - 1], sem_second, (LEVEL1 + child, quarter))

        repeat(SECOND, give)

    @pl.when(is_second)
    def _():
        slot = me - LEVEL1
        for kind in range(3):
            for relay in range(SECOND):
                sub_tables[relay, kind] = tables[kind, relay * SUB:(relay + 1) * SUB, :]

        def give_tables(relay):
            @pl.when(slot != relay)
            def _():
                send(sub_tables.at[relay], relay_tables.at[slot], sem_relay, (LEVEL1 + relay, quarter))

        repeat(SECOND, give_tables)

    for step in range(1, QUARTERS):
        send(own_l0, whole_l0.at[quarter], sem_whole, (me, peer(step)))
    whole_l0[quarter] = own_l0[...]

    @pl.when(is_second)
    def _():
        slot = me - LEVEL1
        relay_tables[slot] = sub_tables[slot]
        await_bytes(relay_measured.at[pl.ds(0, CLIQUES - 1)], sem_measured, 1)
        relay_measured[me] = sub_measured[slot]
        clique = lax.broadcasted_iota(jnp.int32, (CLIQUES, CLIQUES), 0)
        chosen = (clique == targets[...]).astype(jnp.float32)
        for row in range(SUB):
            to_leaf[:, 1, row, :] = jnp.dot(
                chosen, relay_measured[:, row, :],
                precision=lax.Precision.HIGHEST, preferred_element_type=jnp.float32,
            )
        await_bytes(relay_tables.at[pl.ds(0, SECOND - 1)], sem_relay, 1)
        place = quarter * SECOND + slot

        def give_leaf(leaf):
            child = LEVEL2 + leaf
            to_leaf[child, 0] = relay_tables[jnp.maximum(parents[child] - LEVEL1, 0), kinds[child]]
            for other in range(QUARTERS):
                send(to_leaf.at[child], from_relay.at[place], sem_leaf, (child, other))

        repeat(LEAVES, give_leaf)

    await_bytes(whole_l0.at[pl.ds(0, QUARTERS - 1)], sem_whole, 1)

    @pl.when(is_inner)
    def _():
        out[:, 0] = whole_l0[...] + message[...]
        out[:, 1] = jnp.zeros((QUARTERS, ROWS, K), jnp.float32)

    @pl.when(is_leaf)
    def _():
        await_bytes(from_relay, sem_leaf, 1)
        for other in range(QUARTERS):
            for relay in range(SECOND):
                rows = slice(relay * SUB, (relay + 1) * SUB)
                place = other * SECOND + relay
                out[other, 0, rows, :] = whole_l0[other, rows, :] + from_relay[place, 0]
                out[other, 1, rows, :] = from_relay[place, 1]

    await_bytes(partial_in, sem_l0, 0)
    await_bytes(whole_l0.at[pl.ds(0, QUARTERS - 1)], sem_whole, 0)

    @pl.when(is_root)
    def _():
        await_bytes(sub_measured, sem_forward, 0)
        for _ in range(QUARTERS):
            await_bytes(to_first, sem_first, 0)

    @pl.when(is_first)
    def _():
        await_bytes(to_second, sem_second, 0)

    @pl.when(me == 1)
    def _():
        await_bytes(forwarded, sem_measured, 0)

    @pl.when(is_second)
    def _():
        await_bytes(message.at[pl.ds(0, QUARTERS - 1)], sem_rows, 0)
        await_bytes(relay_tables.at[pl.ds(0, SECOND - 1)], sem_relay, 0)
        await_bytes(relay_measured.at[pl.ds(0, SECOND - 1)], sem_measured, 0)
        for _ in range(QUARTERS):
            await_bytes(to_leaf.at[pl.ds(0, LEAVES)], sem_leaf, 0)

    @pl.when(jnp.logical_or(is_first, is_leaf))
    def _():
        await_bytes(sub_measured, sem_measured, 0)


def sweep(parents, kinds, targets, pot, measured):
    hbm, vmem = pl.BlockSpec(memory_space=pltpu.HBM), pl.BlockSpec(memory_space=pltpu.VMEM)
    f32 = jnp.float32
    scratch = [
        (ROWS, K),
        (K, K), (QUARTERS - 1, ROWS, K), (ROWS, K), (QUARTERS, ROWS, K), (QUARTERS, ROWS, K), (K, K), (ROWS, K, K),
        (3, ROWS, K),
        (FIRST, ROWS, K), (SECOND, ROWS, K), (FIRST, ROWS, K), (SECOND, 3, SUB, K), (SECOND, 3, SUB, K),
        (SECOND, SUB, K), (SECOND, SUB, K), (CLIQUES, SUB, K), (CLIQUES, 2, SUB, K), (CLIQUES, 2, SUB, K),
    ]
    return pl.pallas_call(
        sweep_kernel,
        out_shape=(
            jax.ShapeDtypeStruct((QUARTERS, 2, ROWS, K), f32),
            jax.ShapeDtypeStruct((ROWS, K, K), f32),
        ),
        in_specs=[hbm] * 5,
        out_specs=(vmem, vmem),
        scratch_shapes=[
            pltpu.SMEM((CLIQUES,), jnp.int32), pltpu.SMEM((CLIQUES,), jnp.int32), pltpu.VMEM((1, CLIQUES), jnp.int32),
            *(pltpu.VMEM(shape, f32) for shape in scratch),
            pltpu.SemaphoreType.DMA((4,)), pltpu.SemaphoreType.DMA((QUARTERS,)),
            *[pltpu.SemaphoreType.DMA((2,))] * 9,
        ],
        compiler_params=pltpu.CompilerParams(
            collective_id=0, has_side_effects=True, vmem_limit_bytes=16 * 1024 * 1024
        ),
        name="sweep",
    )(parents, kinds, targets, pot, measured)


BLOCK = 8


def finish_kernel(final, pot, marginal_hbm, updated_hbm, marginal, updated, sem):
    me = lax.axis_index("wide")
    quarter = lax.axis_index("narrow")
    cells = final[:, 0]
    largest = jnp.max(cells)
    weights = jnp.exp(cells - largest)
    scale = jnp.float32(K * K) / jnp.sum(weights)
    whole = weights * scale
    marginal[...] = jnp.exp(final[quarter, 0] - largest) * scale
    copies = [pltpu.make_async_copy(marginal, marginal_hbm, sem.at[0])]
    copies[0].start()
    term = jnp.where(me >= LEVEL2, jnp.float32(0.5) * (whole - final[:, 1]), jnp.float32(0.0)).reshape(K, K)
    for block in range(ROWS // BLOCK):
        rows = slice(block * BLOCK, (block + 1) * BLOCK)
        updated[rows] = pot[rows] - term[None]
        copies.append(pltpu.make_async_copy(updated.at[rows], updated_hbm.at[rows], sem.at[1 + block]))
        copies[-1].start()
    for copy in copies:
        copy.wait()


def finish(final, pot):
    hbm, vmem = pl.BlockSpec(memory_space=pltpu.HBM), pl.BlockSpec(memory_space=pltpu.VMEM)
    shapes = (ROWS, K), (ROWS, K, K)
    return pl.pallas_call(
        finish_kernel,
        out_shape=tuple(jax.ShapeDtypeStruct(shape, jnp.float32) for shape in shapes),
        in_specs=[vmem, vmem],
        out_specs=(hbm, hbm),
        scratch_shapes=[*(pltpu.VMEM(shape, jnp.float32) for shape in shapes), pltpu.SemaphoreType.DMA((1 + ROWS // BLOCK,))],
        compiler_params=pltpu.CompilerParams(vmem_limit_bytes=16 * 1024 * 1024),
        name="finish",
    )(final, pot)


def body(potentials, parents, separator_excluded, measurement_clique, measured):
    parents, separator_excluded, measurement_clique, measured, potentials = (
        pltpu.with_memory_space_constraint(array, pltpu.HBM)
        for array in (parents, separator_excluded, measurement_clique[None], measured[0], potentials[0])
    )
    pot = potentials
    final, pot = sweep(parents, separator_excluded, measurement_clique, pot, measured)
    marginal, updated = finish(final, pot)
    return marginal[None], updated[None]


def solution(mesh):
    return jax.shard_map(
        body,
        mesh=mesh,
        in_specs=(P("wide", "narrow", None, None), P(), P(), P(), P("wide", "narrow", None)),
        out_specs=(P("wide", "narrow", None), P("wide", "narrow", None, None)),
        check_vma=False,
    )
```

```python
import jax
import jax.numpy as jnp
from jax import lax
from jax.experimental import pallas as pl
from jax.experimental.pallas import tpu as pltpu
from jax.sharding import PartitionSpec as P

MESH = pl.DeviceIdType.MESH
K = 128
QUARTERS = 4
ROWS = K // QUARTERS
CLIQUES = 64
LEVEL1, LEVEL2 = 5, 21
FIRST = LEVEL1 - 1
SECOND = LEVEL2 - LEVEL1
LEAVES = CLIQUES - LEVEL2
SUB = ROWS // SECOND


def sweep_kernel(
    parents_hbm, kinds_hbm, targets_hbm, pot_hbm, measured_hbm, out, pot,
    parents, kinds, targets, measured,
    partial, partial_in, own_l0, whole_l0, message, message_t, pot_t, tables,
    to_first, to_second, candidates, sub_tables, relay_tables,
    sub_measured, forwarded, relay_measured, measured_to_leaf, whole_measured, to_leaf, from_relay,
    sem_small, sem_pot,
    sem_l0, sem_whole, sem_first, sem_second, sem_rows, sem_relay, sem_forward, sem_measured, sem_given, sem_gather, sem_leaf,
):
    me = lax.axis_index("wide")
    quarter = lax.axis_index("narrow")
    is_root = me == 0
    is_first = jnp.logical_and(me >= 1, me < LEVEL1)
    is_second = jnp.logical_and(me >= LEVEL1, me < LEVEL2)
    is_leaf = me >= LEVEL2
    is_inner = me < LEVEL2
    peers = QUARTERS - 1

    def peer(step):
        return lax.rem(quarter + step, QUARTERS)

    def rows_of(part):
        return pl.ds(pl.multiple_of(part * ROWS, ROWS), ROWS)

    def repeat(count, function, unroll=1):
        def run(index, carry):
            function(index)
            return carry

        lax.fori_loop(0, count, run, 0, unroll=unroll)

    def send(source, target, sem, device):
        pltpu.make_async_remote_copy(
            src_ref=source, dst_ref=target, send_sem=sem.at[0], recv_sem=sem.at[1],
            device_id=device, device_id_type=MESH,
        ).start()

    def await_bytes(like, sem, which):
        pltpu.make_async_copy(like, like, sem.at[which]).wait()

    small = [
        pltpu.make_async_copy(source, target, sem_small.at[index])
        for index, (source, target) in enumerate(
            ((parents_hbm, parents), (kinds_hbm, kinds), (targets_hbm, targets), (measured_hbm, measured))
        )
    ]

    def pot_copy(step):
        rows = rows_of(peer(step))
        return pltpu.make_async_copy(pot_hbm.at[:, rows], pot.at[:, rows], sem_pot.at[step])

    order = (1, 2, 3, 0)
    for step in order:
        pot_copy(step).start()
    for copy in small:
        copy.start()

    barrier = pltpu.get_barrier_semaphore()

    def greet(wide, narrow):
        pl.semaphore_signal(barrier, inc=1, device_id=(wide, narrow), device_id_type=MESH)

    for step in range(1, QUARTERS):
        greet(me, peer(step))

    @pl.when(is_first)
    def _():
        greet(0, quarter)

    @pl.when(is_second)
    def _():
        def one(index):
            greet(1 + index + (index >= me - 1).astype(jnp.int32), quarter)

        repeat(CLIQUES - 2, one)

    @pl.when(is_leaf)
    def _():
        def one(index):
            greet(LEVEL1 + index // QUARTERS, lax.rem(index, QUARTERS))

        repeat(SECOND * QUARTERS, one)

    def partial_lse(step):
        base = peer(step) * ROWS

        def one(block):
            rows = pl.ds(pl.multiple_of(base + block * 8, 8), 8)
            slab = pot[:, rows, :]
            largest = jnp.max(slab, axis=0)
            partial[rows, :] = largest + jnp.log(jnp.sum(jnp.exp(slab - largest[None]), axis=0))

        pot_copy(step).wait()
        repeat(ROWS // 8, one, unroll=2)

    partial_lse(1)

    @pl.when(is_root)
    def _():
        pl.semaphore_wait(barrier, peers + FIRST)

    @pl.when(is_first)
    def _():
        pl.semaphore_wait(barrier, peers + SECOND)

    @pl.when(is_leaf)
    def _():
        pl.semaphore_wait(barrier, peers + SECOND)

    @pl.when(is_second)
    def _():
        pl.semaphore_wait(barrier, peers + SECOND - 1 + LEAVES * QUARTERS)

    for step in order:
        if step != order[0]:
            partial_lse(step)
        if step:
            send(partial.at[rows_of(peer(step))], partial_in.at[step - 1], sem_l0, (me, peer(step)))

    for copy in small:
        copy.wait()
    for relay in range(SECOND):
        sub_measured[relay] = measured[relay * SUB:(relay + 1) * SUB, :]

    @pl.when(is_root)
    def _():
        send(sub_measured, forwarded, sem_forward, (1, quarter))

    @pl.when(jnp.logical_not(is_root))
    def _():
        def give(relay):
            @pl.when(me != LEVEL1 + relay)
            def _():
                send(sub_measured.at[relay], relay_measured.at[me], sem_measured, (LEVEL1 + relay, quarter))

        repeat(SECOND, give)

    @pl.when(me == 1)
    def _():
        await_bytes(forwarded, sem_forward, 1)

        def give(relay):
            send(forwarded.at[relay], relay_measured.at[0], sem_measured, (LEVEL1 + relay, quarter))

        repeat(SECOND, give)

    @pl.when(is_inner)
    def _():
        def turn(a0):
            pot_t[a0] = pot[a0].T

        repeat(ROWS, turn, unroll=4)

    @pl.when(is_second)
    def _():
        slot = me - LEVEL1
        await_bytes(relay_measured.at[pl.ds(0, CLIQUES - 1)], sem_measured, 1)
        relay_measured[me] = sub_measured[slot]
        clique = lax.broadcasted_iota(jnp.int32, (CLIQUES, CLIQUES), 0)
        chosen = (clique == targets[...]).astype(jnp.float32)
        for row in range(SUB):
            measured_to_leaf[:, row, :] = jnp.dot(
                chosen, relay_measured[:, row, :],
                precision=lax.Precision.HIGHEST, preferred_element_type=jnp.float32,
            )

        def give(leaf):
            child = LEVEL2 + leaf
            send(measured_to_leaf.at[child], whole_measured.at[quarter, slot], sem_given, (child, quarter))

        repeat(LEAVES, give)

    @pl.when(is_root)
    def _():
        message[...] = jnp.zeros_like(message)

    @pl.when(is_first)
    def _():
        await_bytes(message, sem_first, 1)

    @pl.when(is_second)
    def _():
        await_bytes(candidates, sem_second, 1)
        message[quarter] = candidates[jnp.maximum(parents[me] - 1, 0)]
        for step in range(1, QUARTERS):
            send(message.at[quarter], message.at[quarter], sem_rows, (me, peer(step)))
        await_bytes(message.at[pl.ds(0, QUARTERS - 1)], sem_rows, 1)

    @pl.when(is_inner)
    def _():
        for other in range(QUARTERS):
            message_t[:, other * ROWS:(other + 1) * ROWS] = message[other].T

        def eight(group):
            rows = pl.ds(pl.multiple_of(group * 8, 8), 8)
            for kind in (1, 2):
                tops, totals = [], []
                for step in range(8):
                    a0 = group * 8 + step
                    if kind == 1:
                        belief = (pot[a0].reshape(QUARTERS, ROWS, K) + message[...]).reshape(K, K)
                    else:
                        belief = pot_t[a0] + message_t[...]
                    largest = jnp.max(belief, axis=0, keepdims=True)
                    tops.append(largest)
                    totals.append(jnp.sum(jnp.exp(belief - largest), axis=0, keepdims=True))
                tables[kind, rows, :] = jnp.concatenate(tops, 0) + jnp.log(jnp.concatenate(totals, 0))

        repeat(ROWS // 8, eight)

    await_bytes(partial_in, sem_l0, 1)
    mine = partial[rows_of(quarter), :]
    largest = jnp.maximum(mine, jnp.max(partial_in[...], axis=0))
    summed = jnp.exp(mine - largest) + jnp.sum(jnp.exp(partial_in[...] - largest[None]), axis=0)
    own_l0[...] = largest + jnp.log(summed)

    @pl.when(is_inner)
    def _():
        tables[0] = own_l0[...] + message[quarter]

    @pl.when(is_root)
    def _():
        for child in range(FIRST):
            to_first[child] = tables[kinds[1 + child]]
            for other in range(QUARTERS):
                send(to_first.at[child], message.at[quarter], sem_first, (1 + child, other))

    @pl.when(is_first)
    def _():
        def give(child):
            to_second[child] = tables[kinds[LEVEL1 + child]]
            send(to_second.at[child], candidates.at[me - 1], sem_second, (LEVEL1 + child, quarter))

        repeat(SECOND, give)

    @pl.when(is_second)
    def _():
        slot = me - LEVEL1
        for kind in range(3):
            for relay in range(SECOND):
                sub_tables[relay, kind] = tables[kind, relay * SUB:(relay + 1) * SUB, :]

        def give_tables(relay):
            @pl.when(slot != relay)
            def _():
                send(sub_tables.at[relay], relay_tables.at[slot], sem_relay, (LEVEL1 + relay, quarter))

        repeat(SECOND, give_tables)

    for step in range(1, QUARTERS):
        send(own_l0, whole_l0.at[quarter], sem_whole, (me, peer(step)))
    whole_l0[quarter] = own_l0[...]

    @pl.when(is_second)
    def _():
        slot = me - LEVEL1
        relay_tables[slot] = sub_tables[slot]
        await_bytes(relay_tables.at[pl.ds(0, SECOND - 1)], sem_relay, 1)
        place = quarter * SECOND + slot

        def give_leaf(leaf):
            child = LEVEL2 + leaf
            to_leaf[leaf] = relay_tables[jnp.maximum(parents[child] - LEVEL1, 0), kinds[child]]
            for other in range(QUARTERS):
                send(to_leaf.at[leaf], from_relay.at[place], sem_leaf, (child, other))

        repeat(LEAVES, give_leaf)

    await_bytes(whole_l0.at[pl.ds(0, QUARTERS - 1)], sem_whole, 1)

    @pl.when(is_inner)
    def _():
        out[:, 0] = whole_l0[...] + message[...]
        out[:, 1] = jnp.zeros((QUARTERS, ROWS, K), jnp.float32)

    @pl.when(is_leaf)
    def _():
        await_bytes(whole_measured.at[0], sem_given, 1)
        for step in range(1, QUARTERS):
            send(whole_measured.at[quarter], whole_measured.at[quarter], sem_gather, (me, peer(step)))
        await_bytes(whole_measured.at[pl.ds(0, QUARTERS - 1)], sem_gather, 1)
        for other in range(QUARTERS):
            for relay in range(SECOND):
                out[other, 1, relay * SUB:(relay + 1) * SUB, :] = whole_measured[other, relay]
        await_bytes(from_relay, sem_leaf, 1)
        for other in range(QUARTERS):
            for relay in range(SECOND):
                rows = slice(relay * SUB, (relay + 1) * SUB)
                place = other * SECOND + relay
                out[other, 0, rows, :] = whole_l0[other, rows, :] + from_relay[place]

    await_bytes(partial_in, sem_l0, 0)
    await_bytes(whole_l0.at[pl.ds(0, QUARTERS - 1)], sem_whole, 0)

    @pl.when(is_root)
    def _():
        await_bytes(sub_measured, sem_forward, 0)
        for _ in range(QUARTERS):
            await_bytes(to_first, sem_first, 0)

    @pl.when(is_first)
    def _():
        await_bytes(to_second, sem_second, 0)

    @pl.when(me == 1)
    def _():
        await_bytes(forwarded, sem_measured, 0)

    @pl.when(is_second)
    def _():
        await_bytes(message.at[pl.ds(0, QUARTERS - 1)], sem_rows, 0)
        await_bytes(relay_tables.at[pl.ds(0, SECOND - 1)], sem_relay, 0)
        await_bytes(relay_measured.at[pl.ds(0, SECOND - 1)], sem_measured, 0)
        await_bytes(measured_to_leaf.at[pl.ds(0, LEAVES)], sem_given, 0)
        for _ in range(QUARTERS):
            await_bytes(to_leaf, sem_leaf, 0)

    @pl.when(is_leaf)
    def _():
        await_bytes(whole_measured.at[pl.ds(0, QUARTERS - 1)], sem_gather, 0)

    @pl.when(jnp.logical_or(is_first, is_leaf))
    def _():
        await_bytes(sub_measured, sem_measured, 0)


def sweep(parents, kinds, targets, pot, measured):
    hbm, vmem = pl.BlockSpec(memory_space=pltpu.HBM), pl.BlockSpec(memory_space=pltpu.VMEM)
    f32 = jnp.float32
    scratch = [
        (ROWS, K),
        (K, K), (QUARTERS - 1, ROWS, K), (ROWS, K), (QUARTERS, ROWS, K), (QUARTERS, ROWS, K), (K, K), (ROWS, K, K),
        (3, ROWS, K),
        (FIRST, ROWS, K), (SECOND, ROWS, K), (FIRST, ROWS, K), (SECOND, 3, SUB, K), (SECOND, 3, SUB, K),
        (SECOND, SUB, K), (SECOND, SUB, K), (CLIQUES, SUB, K), (CLIQUES, SUB, K), (QUARTERS, SECOND, SUB, K),
        (LEAVES, SUB, K), (CLIQUES, SUB, K),
    ]
    return pl.pallas_call(
        sweep_kernel,
        out_shape=(
            jax.ShapeDtypeStruct((QUARTERS, 2, ROWS, K), f32),
            jax.ShapeDtypeStruct((ROWS, K, K), f32),
        ),
        in_specs=[hbm] * 5,
        out_specs=(vmem, vmem),
        scratch_shapes=[
            pltpu.SMEM((CLIQUES,), jnp.int32), pltpu.SMEM((CLIQUES,), jnp.int32), pltpu.VMEM((1, CLIQUES), jnp.int32),
            *(pltpu.VMEM(shape, f32) for shape in scratch),
            pltpu.SemaphoreType.DMA((4,)), pltpu.SemaphoreType.DMA((QUARTERS,)),
            *[pltpu.SemaphoreType.DMA((2,))] * 11,
        ],
        compiler_params=pltpu.CompilerParams(
            collective_id=0, has_side_effects=True, vmem_limit_bytes=16 * 1024 * 1024
        ),
        name="sweep",
    )(parents, kinds, targets, pot, measured)


BLOCK = 8


def finish_kernel(final, pot, marginal_hbm, updated_hbm, marginal, updated, sem):
    me = lax.axis_index("wide")
    quarter = lax.axis_index("narrow")
    cells = final[:, 0]
    largest = jnp.max(cells)
    weights = jnp.exp(cells - largest)
    scale = jnp.float32(K * K) / jnp.sum(weights)
    whole = weights * scale
    marginal[...] = jnp.exp(final[quarter, 0] - largest) * scale
    copies = [pltpu.make_async_copy(marginal, marginal_hbm, sem.at[0])]
    copies[0].start()
    term = jnp.where(me >= LEVEL2, jnp.float32(0.5) * (whole - final[:, 1]), jnp.float32(0.0)).reshape(K, K)
    for block in range(ROWS // BLOCK):
        rows = slice(block * BLOCK, (block + 1) * BLOCK)
        updated[rows] = pot[rows] - term[None]
        copies.append(pltpu.make_async_copy(updated.at[rows], updated_hbm.at[rows], sem.at[1 + block]))
        copies[-1].start()
    for copy in copies:
        copy.wait()


def finish(final, pot):
    hbm, vmem = pl.BlockSpec(memory_space=pltpu.HBM), pl.BlockSpec(memory_space=pltpu.VMEM)
    shapes = (ROWS, K), (ROWS, K, K)
    return pl.pallas_call(
        finish_kernel,
        out_shape=tuple(jax.ShapeDtypeStruct(shape, jnp.float32) for shape in shapes),
        in_specs=[vmem, vmem],
        out_specs=(hbm, hbm),
        scratch_shapes=[*(pltpu.VMEM(shape, jnp.float32) for shape in shapes), pltpu.SemaphoreType.DMA((1 + ROWS // BLOCK,))],
        compiler_params=pltpu.CompilerParams(vmem_limit_bytes=16 * 1024 * 1024),
        name="finish",
    )(final, pot)


def body(potentials, parents, separator_excluded, measurement_clique, measured):
    parents, separator_excluded, measurement_clique, measured, potentials = (
        pltpu.with_memory_space_constraint(array, pltpu.HBM)
        for array in (parents, separator_excluded, measurement_clique[None], measured[0], potentials[0])
    )
    pot = potentials
    final, pot = sweep(parents, separator_excluded, measurement_clique, pot, measured)
    marginal, updated = finish(final, pot)
    return marginal[None], updated[None]


def solution(mesh):
    return jax.shard_map(
        body,
        mesh=mesh,
        in_specs=(P("wide", "narrow", None, None), P(), P(), P(), P("wide", "narrow", None)),
        out_specs=(P("wide", "narrow", None), P("wide", "narrow", None, None)),
        check_vma=False,
    )
```

```python
import jax
import jax.numpy as jnp
from jax import lax
from jax.experimental import pallas as pl
from jax.experimental.pallas import tpu as pltpu
from jax.sharding import PartitionSpec as P

MESH = pl.DeviceIdType.MESH
K = 128
QUARTERS = 4
ROWS = K // QUARTERS
CLIQUES = 64
LEVEL1, LEVEL2 = 5, 21
FIRST = LEVEL1 - 1
SECOND = LEVEL2 - LEVEL1
LEAVES = CLIQUES - LEVEL2
RELAYS = 16
FRONT = 2 * RELAYS
SUB = ROWS // RELAYS


def sweep_kernel(
    parents_hbm, kinds_hbm, targets_hbm, pot_hbm, measured_hbm, out, pot,
    parents, kinds, targets, measured,
    partial, partial_in, own_l0, whole_l0, message, message_t, pot_t, tables,
    to_first, to_second, candidates, sub_tables, relay_tables,
    sub_measured, forwarded, relay_measured, measured_to_leaf, whole_measured, to_leaf, from_relay,
    sem_small, sem_pot,
    sem_l0, sem_whole, sem_first, sem_second, sem_rows, sem_relay, sem_forward, sem_measured, sem_given, sem_gather, sem_leaf,
    sem_near, sem_far,
):
    me = lax.axis_index("wide")
    quarter = lax.axis_index("narrow")
    is_root = me == 0
    is_first = jnp.logical_and(me >= 1, me < LEVEL1)
    is_second = jnp.logical_and(me >= LEVEL1, me < LEVEL2)
    is_leaf = me >= LEVEL2
    is_inner = me < LEVEL2
    odd = lax.rem(me, 2)
    is_relay = jnp.logical_and(odd == 1, me < FRONT)
    is_early = me < LEVEL1
    peers = QUARTERS - 1

    def peer(step):
        return lax.rem(quarter + step, QUARTERS)

    def rows_of(part):
        return pl.ds(pl.multiple_of(part * ROWS, ROWS), ROWS)

    def repeat(count, function, unroll=1):
        def run(index, carry):
            function(index)
            return carry

        lax.fori_loop(0, count, run, 0, unroll=unroll)

    def send(source, target, sem, device):
        pltpu.make_async_remote_copy(
            src_ref=source, dst_ref=target, send_sem=sem.at[0], recv_sem=sem.at[1],
            device_id=device, device_id_type=MESH,
        ).start()

    def await_bytes(like, sem, which):
        pltpu.make_async_copy(like, like, sem.at[which]).wait()

    small = [
        pltpu.make_async_copy(source, target, sem_small.at[index])
        for index, (source, target) in enumerate(
            ((parents_hbm, parents), (kinds_hbm, kinds), (targets_hbm, targets), (measured_hbm, measured))
        )
    ]

    def pot_copy(step):
        rows = rows_of(peer(step))
        return pltpu.make_async_copy(pot_hbm.at[:, rows], pot.at[:, rows], sem_pot.at[step])

    order = (1, 2, 3, 0)
    far_first = (2, 1, 3, 0)
    for step in order:
        pot_copy(step).start()
    for copy in small:
        copy.start()

    barrier = pltpu.get_barrier_semaphore()

    def greet(wide, narrow):
        pl.semaphore_signal(barrier, inc=1, device_id=(wide, narrow), device_id_type=MESH)

    for step in range(1, QUARTERS):
        greet(me, peer(step))

    @pl.when(is_root)
    def _():
        for child in range(1, LEVEL1):
            greet(child, quarter)

    @pl.when(is_first)
    def _():
        for step in range(FIRST - 1):
            greet(1 + lax.rem(me + step, FIRST), quarter)
        repeat(FRONT - LEVEL1, lambda index: greet(LEVEL1 + index, quarter))

    @pl.when(jnp.logical_and(is_first, is_relay))
    def _():
        repeat(CLIQUES - FRONT, lambda index: greet(FRONT + index, quarter))

    @pl.when(jnp.logical_and(jnp.logical_not(is_early), is_relay))
    def _():
        def one(index):
            greet(LEVEL1 + index + (index >= me - LEVEL1).astype(jnp.int32), quarter)

        repeat(CLIQUES - LEVEL1 - 1, one)

    def partial_lse(step):
        base = peer(step) * ROWS

        def one(block):
            rows = pl.ds(pl.multiple_of(base + block * 8, 8), 8)
            slab = pot[:, rows, :]
            largest = jnp.max(slab, axis=0)
            partial[rows, :] = largest + jnp.log(jnp.sum(jnp.exp(slab - largest[None]), axis=0))

        pot_copy(step).wait()
        repeat(ROWS // 8, one, unroll=2)

    partial_lse(1)

    @pl.when(is_root)
    def _():
        pl.semaphore_wait(barrier, peers)

    @pl.when(is_first)
    def _():
        pl.semaphore_wait(barrier, peers + FIRST)
        pl.semaphore_signal(sem_near, inc=1, device_id=(0, quarter), device_id_type=MESH)

    @pl.when(jnp.logical_and(jnp.logical_not(is_early), me < FRONT))
    def _():
        pl.semaphore_wait(barrier, peers + RELAYS - odd + 2)
        for child in range(1, LEVEL1):
            pl.semaphore_signal(sem_far, inc=1, device_id=(child, quarter), device_id_type=MESH)

    @pl.when(me >= FRONT)
    def _():
        pl.semaphore_wait(barrier, peers + RELAYS)

    for step in order:
        if step != order[0]:
            partial_lse(step)
        if step:
            send(partial.at[rows_of(peer(step))], partial_in.at[step - 1], sem_l0, (me, peer(step)))

    for copy in small:
        copy.wait()
    for relay in range(RELAYS):
        sub_measured[relay] = measured[relay * SUB:(relay + 1) * SUB, :]

    def give_measured(relay):
        @pl.when(me != 2 * relay + 1)
        def _():
            send(sub_measured.at[relay], relay_measured.at[me], sem_measured, (2 * relay + 1, quarter))

    @pl.when(jnp.logical_not(is_early))
    def _():
        repeat(RELAYS, give_measured)

    @pl.when(is_inner)
    def _():
        def turn(a0):
            pot_t[a0] = pot[a0].T

        repeat(ROWS, turn, unroll=4)

    @pl.when(is_root)
    def _():
        message[...] = jnp.zeros_like(message)

    @pl.when(is_first)
    def _():
        await_bytes(message, sem_first, 1)

    @pl.when(is_second)
    def _():
        await_bytes(candidates, sem_second, 1)
        message[quarter] = candidates[jnp.maximum(parents[me] - 1, 0)]
        for step in range(1, QUARTERS):
            send(message.at[quarter], message.at[quarter], sem_rows, (me, peer(step)))
        await_bytes(message.at[pl.ds(0, QUARTERS - 1)], sem_rows, 1)

    @pl.when(is_inner)
    def _():
        for other in range(QUARTERS):
            message_t[:, other * ROWS:(other + 1) * ROWS] = message[other].T

        def eight(group):
            rows = pl.ds(pl.multiple_of(group * 8, 8), 8)
            for kind in (1, 2):
                tops, totals = [], []
                for step in range(8):
                    a0 = group * 8 + step
                    if kind == 1:
                        belief = (pot[a0].reshape(QUARTERS, ROWS, K) + message[...]).reshape(K, K)
                    else:
                        belief = pot_t[a0] + message_t[...]
                    largest = jnp.max(belief, axis=0, keepdims=True)
                    tops.append(largest)
                    totals.append(jnp.sum(jnp.exp(belief - largest), axis=0, keepdims=True))
                tables[kind, rows, :] = jnp.concatenate(tops, 0) + jnp.log(jnp.concatenate(totals, 0))

        repeat(ROWS // 8, eight)

    await_bytes(partial_in, sem_l0, 1)
    mine = partial[rows_of(quarter), :]
    largest = jnp.maximum(mine, jnp.max(partial_in[...], axis=0))
    summed = jnp.exp(mine - largest) + jnp.sum(jnp.exp(partial_in[...] - largest[None]), axis=0)
    own_l0[...] = largest + jnp.log(summed)

    @pl.when(is_inner)
    def _():
        tables[0] = own_l0[...] + message[quarter]

    @pl.when(is_root)
    def _():
        pl.semaphore_wait(sem_near, FIRST)
        for child in reversed(range(FIRST)):
            to_first[child] = tables[kinds[1 + child]]
            for step in far_first:
                send(to_first.at[child], message.at[quarter], sem_first, (1 + child, peer(step)))
        send(sub_measured, forwarded, sem_forward, (1, quarter))

    @pl.when(is_first)
    def _():
        pl.semaphore_wait(sem_far, FRONT - LEVEL1)

        def give(index):
            child = lax.rem(index + 3, SECOND)
            to_second[child] = tables[kinds[LEVEL1 + child]]
            send(to_second.at[child], candidates.at[me - 1], sem_second, (LEVEL1 + child, quarter))

        repeat(SECOND, give)
        repeat(RELAYS, give_measured)

    @pl.when(me == 1)
    def _():
        await_bytes(forwarded, sem_forward, 1)

        def give(index):
            relay = 1 + index
            send(forwarded.at[relay], relay_measured.at[0], sem_measured, (2 * relay + 1, quarter))

        repeat(RELAYS - 1, give)
        relay_measured[0] = forwarded[0]

    @pl.when(is_second)
    def _():
        slot = me - LEVEL1
        for kind in range(3):
            for relay in range(RELAYS):
                sub_tables[relay, kind] = tables[kind, relay * SUB:(relay + 1) * SUB, :]

        def give_tables(relay):
            @pl.when(me != 2 * relay + 1)
            def _():
                send(sub_tables.at[relay], relay_tables.at[slot], sem_relay, (2 * relay + 1, quarter))

        repeat(RELAYS, give_tables)

    for step in range(1, QUARTERS):
        send(own_l0, whole_l0.at[quarter], sem_whole, (me, peer(step)))
    whole_l0[quarter] = own_l0[...]

    relay_slot = me // 2

    @pl.when(me == 1)
    def _():
        await_bytes(relay_measured.at[pl.ds(0, CLIQUES - 2)], sem_measured, 1)

    @pl.when(jnp.logical_and(is_relay, me != 1))
    def _():
        await_bytes(relay_measured.at[pl.ds(0, CLIQUES - 1)], sem_measured, 1)

    @pl.when(is_relay)
    def _():
        relay_measured[me] = sub_measured[relay_slot]
        clique = lax.broadcasted_iota(jnp.int32, (CLIQUES, CLIQUES), 0)
        chosen = (clique == targets[...]).astype(jnp.float32)
        for row in range(SUB):
            measured_to_leaf[:, row, :] = jnp.dot(
                chosen, relay_measured[:, row, :],
                precision=lax.Precision.HIGHEST, preferred_element_type=jnp.float32,
            )

        def give(leaf):
            child = LEVEL2 + leaf

            @pl.when(child != me)
            def _():
                send(measured_to_leaf.at[child], whole_measured.at[quarter, relay_slot], sem_given, (child, quarter))

        repeat(LEAVES, give)

    @pl.when(jnp.logical_and(is_relay, is_second))
    def _():
        relay_tables[me - LEVEL1] = sub_tables[relay_slot]
        await_bytes(relay_tables.at[pl.ds(0, SECOND - 1)], sem_relay, 1)

    @pl.when(jnp.logical_and(is_relay, jnp.logical_not(is_second)))
    def _():
        await_bytes(relay_tables, sem_relay, 1)

    @pl.when(is_relay)
    def _():
        place = quarter * RELAYS + relay_slot

        def give_leaf(index):
            leaf = lax.rem(index * (LEAVES // 2), LEAVES)
            child = LEVEL2 + leaf
            to_leaf[leaf] = relay_tables[jnp.maximum(parents[child] - LEVEL1, 0), kinds[child]]
            for step in far_first[:-1]:
                send(to_leaf.at[leaf], from_relay.at[place], sem_leaf, (child, peer(step)))

            @pl.when(child != me)
            def _():
                send(to_leaf.at[leaf], from_relay.at[place], sem_leaf, (child, quarter))

        repeat(LEAVES, give_leaf)

    is_both = jnp.logical_and(is_relay, is_leaf)
    is_plain_leaf = jnp.logical_and(is_leaf, jnp.logical_not(is_relay))

    @pl.when(is_both)
    def _():
        whole_measured[quarter, relay_slot] = measured_to_leaf[me]
        from_relay[quarter * RELAYS + relay_slot] = to_leaf[me - LEVEL2]
        await_bytes(whole_measured.at[0, pl.ds(0, RELAYS - 1)], sem_given, 1)

    @pl.when(is_plain_leaf)
    def _():
        await_bytes(whole_measured.at[0], sem_given, 1)

    await_bytes(whole_l0.at[pl.ds(0, QUARTERS - 1)], sem_whole, 1)

    @pl.when(is_inner)
    def _():
        out[:, 0] = whole_l0[...] + message[...]
        out[:, 1] = jnp.zeros((QUARTERS, ROWS, K), jnp.float32)

    @pl.when(is_leaf)
    def _():
        for step in range(1, QUARTERS):
            send(whole_measured.at[quarter], whole_measured.at[quarter], sem_gather, (me, peer(step)))
        await_bytes(whole_measured.at[pl.ds(0, QUARTERS - 1)], sem_gather, 1)
        for other in range(QUARTERS):
            for relay in range(RELAYS):
                out[other, 1, relay * SUB:(relay + 1) * SUB, :] = whole_measured[other, relay]

    @pl.when(is_both)
    def _():
        await_bytes(from_relay.at[pl.ds(0, CLIQUES - 1)], sem_leaf, 1)

    @pl.when(is_plain_leaf)
    def _():
        await_bytes(from_relay, sem_leaf, 1)

    @pl.when(is_leaf)
    def _():
        for other in range(QUARTERS):
            for relay in range(RELAYS):
                rows = slice(relay * SUB, (relay + 1) * SUB)
                out[other, 0, rows, :] = whole_l0[other, rows, :] + from_relay[other * RELAYS + relay]

    await_bytes(partial_in, sem_l0, 0)
    await_bytes(whole_l0.at[pl.ds(0, QUARTERS - 1)], sem_whole, 0)

    @pl.when(is_root)
    def _():
        await_bytes(sub_measured, sem_forward, 0)
        for _ in range(QUARTERS):
            await_bytes(to_first, sem_first, 0)

    @pl.when(is_first)
    def _():
        await_bytes(to_second, sem_second, 0)

    @pl.when(me == 1)
    def _():
        await_bytes(forwarded.at[pl.ds(0, RELAYS - 1)], sem_measured, 0)

    @pl.when(is_second)
    def _():
        await_bytes(message.at[pl.ds(0, QUARTERS - 1)], sem_rows, 0)

    @pl.when(jnp.logical_and(is_second, is_relay))
    def _():
        await_bytes(sub_tables.at[pl.ds(0, RELAYS - 1)], sem_relay, 0)

    @pl.when(jnp.logical_and(is_second, jnp.logical_not(is_relay)))
    def _():
        await_bytes(sub_tables, sem_relay, 0)

    @pl.when(is_relay)
    def _():
        await_bytes(sub_measured.at[pl.ds(0, RELAYS - 1)], sem_measured, 0)
        for _ in range(QUARTERS - 1):
            await_bytes(to_leaf, sem_leaf, 0)

    @pl.when(is_both)
    def _():
        await_bytes(measured_to_leaf.at[pl.ds(0, LEAVES - 1)], sem_given, 0)
        await_bytes(to_leaf.at[pl.ds(0, LEAVES - 1)], sem_leaf, 0)

    @pl.when(jnp.logical_and(is_relay, is_inner))
    def _():
        await_bytes(measured_to_leaf.at[pl.ds(0, LEAVES)], sem_given, 0)
        await_bytes(to_leaf, sem_leaf, 0)

    @pl.when(is_leaf)
    def _():
        await_bytes(whole_measured.at[pl.ds(0, QUARTERS - 1)], sem_gather, 0)

    @pl.when(jnp.logical_not(jnp.logical_or(is_root, is_relay)))
    def _():
        await_bytes(sub_measured, sem_measured, 0)


def sweep(parents, kinds, targets, pot, measured):
    hbm, vmem = pl.BlockSpec(memory_space=pltpu.HBM), pl.BlockSpec(memory_space=pltpu.VMEM)
    f32 = jnp.float32
    scratch = [
        (ROWS, K),
        (K, K), (QUARTERS - 1, ROWS, K), (ROWS, K), (QUARTERS, ROWS, K), (QUARTERS, ROWS, K), (K, K), (ROWS, K, K),
        (3, ROWS, K),
        (FIRST, ROWS, K), (SECOND, ROWS, K), (FIRST, ROWS, K), (RELAYS, 3, SUB, K), (SECOND, 3, SUB, K),
        (RELAYS, SUB, K), (RELAYS, SUB, K), (CLIQUES, SUB, K), (CLIQUES, SUB, K), (QUARTERS, RELAYS, SUB, K),
        (LEAVES, SUB, K), (QUARTERS * RELAYS, SUB, K),
    ]
    return pl.pallas_call(
        sweep_kernel,
        out_shape=(
            jax.ShapeDtypeStruct((QUARTERS, 2, ROWS, K), f32),
            jax.ShapeDtypeStruct((ROWS, K, K), f32),
        ),
        in_specs=[hbm] * 5,
        out_specs=(vmem, vmem),
        scratch_shapes=[
            pltpu.SMEM((CLIQUES,), jnp.int32), pltpu.SMEM((CLIQUES,), jnp.int32), pltpu.VMEM((1, CLIQUES), jnp.int32),
            *(pltpu.VMEM(shape, f32) for shape in scratch),
            pltpu.SemaphoreType.DMA((4,)), pltpu.SemaphoreType.DMA((QUARTERS,)),
            *[pltpu.SemaphoreType.DMA((2,))] * 11,
            pltpu.SemaphoreType.REGULAR, pltpu.SemaphoreType.REGULAR,
        ],
        compiler_params=pltpu.CompilerParams(
            collective_id=0, has_side_effects=True, vmem_limit_bytes=16 * 1024 * 1024
        ),
        name="sweep",
    )(parents, kinds, targets, pot, measured)


BLOCK = 8


def finish_kernel(final, pot, marginal_hbm, updated_hbm, marginal, updated, sem):
    me = lax.axis_index("wide")
    quarter = lax.axis_index("narrow")
    cells = final[:, 0]
    largest = jnp.max(cells)
    weights = jnp.exp(cells - largest)
    scale = jnp.float32(K * K) / jnp.sum(weights)
    whole = weights * scale
    marginal[...] = jnp.exp(final[quarter, 0] - largest) * scale
    copies = [pltpu.make_async_copy(marginal, marginal_hbm, sem.at[0])]
    copies[0].start()
    term = jnp.where(me >= LEVEL2, jnp.float32(0.5) * (whole - final[:, 1]), jnp.float32(0.0)).reshape(K, K)
    for block in range(ROWS // BLOCK):
        rows = slice(block * BLOCK, (block + 1) * BLOCK)
        updated[rows] = pot[rows] - term[None]
        copies.append(pltpu.make_async_copy(updated.at[rows], updated_hbm.at[rows], sem.at[1 + block]))
        copies[-1].start()
    for copy in copies:
        copy.wait()


def finish(final, pot):
    hbm, vmem = pl.BlockSpec(memory_space=pltpu.HBM), pl.BlockSpec(memory_space=pltpu.VMEM)
    shapes = (ROWS, K), (ROWS, K, K)
    return pl.pallas_call(
        finish_kernel,
        out_shape=tuple(jax.ShapeDtypeStruct(shape, jnp.float32) for shape in shapes),
        in_specs=[vmem, vmem],
        out_specs=(hbm, hbm),
        scratch_shapes=[*(pltpu.VMEM(shape, jnp.float32) for shape in shapes), pltpu.SemaphoreType.DMA((1 + ROWS // BLOCK,))],
        compiler_params=pltpu.CompilerParams(vmem_limit_bytes=16 * 1024 * 1024),
        name="finish",
    )(final, pot)


def body(potentials, parents, separator_excluded, measurement_clique, measured):
    parents, separator_excluded, measurement_clique, measured, potentials = (
        pltpu.with_memory_space_constraint(array, pltpu.HBM)
        for array in (parents, separator_excluded, measurement_clique[None], measured[0], potentials[0])
    )
    pot = potentials
    final, pot = sweep(parents, separator_excluded, measurement_clique, pot, measured)
    marginal, updated = finish(final, pot)
    return marginal[None], updated[None]


def solution(mesh):
    return jax.shard_map(
        body,
        mesh=mesh,
        in_specs=(P("wide", "narrow", None, None), P(), P(), P(), P("wide", "narrow", None)),
        out_specs=(P("wide", "narrow", None), P("wide", "narrow", None, None)),
        check_vma=False,
    )
```

```python
import jax
import jax.numpy as jnp
from jax import lax
from jax.experimental import pallas as pl
from jax.experimental.pallas import tpu as pltpu
from jax.sharding import PartitionSpec as P

MESH = pl.DeviceIdType.MESH
K = 128
QUARTERS = 4
ROWS = K // QUARTERS
CLIQUES = 64
LEVEL1, LEVEL2 = 5, 21
FIRST = LEVEL1 - 1
SECOND = LEVEL2 - LEVEL1
LEAVES = CLIQUES - LEVEL2
RELAYS = 16
FRONT = 2 * RELAYS
SUB = ROWS // RELAYS
CHIPS, PLANES = 8, 3


def sweep_kernel(
    parents_hbm, kinds_hbm, targets_hbm, pot_hbm, measured_hbm, out, pot,
    parents, kinds, targets, measured,
    partial, partial_in, own_l0, whole_l0, message, message_t, pot_t, tables,
    to_first, to_second, candidates, sub_tables, relay_tables,
    sub_measured, forwarded, relay_measured, measured_to_leaf, whole_measured, to_leaf, from_relay,
    sem_small, sem_pot,
    sem_l0, sem_whole, sem_first, sem_second, sem_rows, sem_relay, sem_forward, sem_measured, sem_given, sem_gather, sem_leaf,
    sem_near, sem_far,
):
    me = lax.axis_index("wide")
    quarter = lax.axis_index("narrow")
    is_root = me == 0
    is_first = jnp.logical_and(me >= 1, me < LEVEL1)
    is_second = jnp.logical_and(me >= LEVEL1, me < LEVEL2)
    is_leaf = me >= LEVEL2
    is_inner = me < LEVEL2
    odd = lax.rem(me, 2)
    is_relay = jnp.logical_and(odd == 1, me < FRONT)
    is_early = me < LEVEL1
    peers = QUARTERS - 1

    def peer(step):
        return lax.rem(quarter + step, QUARTERS)

    def rows_of(part):
        return pl.ds(pl.multiple_of(part * ROWS, ROWS), ROWS)

    def repeat(count, function, unroll=1):
        def run(index, carry):
            function(index)
            return carry

        lax.fori_loop(0, count, run, 0, unroll=unroll)

    def send(source, target, sem, device):
        pltpu.make_async_remote_copy(
            src_ref=source, dst_ref=target, send_sem=sem.at[0], recv_sem=sem.at[1],
            device_id=device, device_id_type=MESH,
        ).start()

    def await_bytes(like, sem, which):
        pltpu.make_async_copy(like, like, sem.at[which]).wait()

    small = [
        pltpu.make_async_copy(source, target, sem_small.at[index])
        for index, (source, target) in enumerate(
            ((parents_hbm, parents), (kinds_hbm, kinds), (targets_hbm, targets), (measured_hbm, measured))
        )
    ]

    def pot_copy(step):
        rows = rows_of(peer(step))
        return pltpu.make_async_copy(pot_hbm.at[:, rows], pot.at[:, rows], sem_pot.at[step])

    order = (1, 2, 3, 0)
    far_first = (2, 1, 3, 0)
    for step in order:
        pot_copy(step).start()
    for copy in small:
        copy.start()

    barrier = pltpu.get_barrier_semaphore()

    def greet(wide, narrow):
        pl.semaphore_signal(barrier, inc=1, device_id=(wide, narrow), device_id_type=MESH)

    for step in range(1, QUARTERS):
        greet(me, peer(step))

    @pl.when(is_root)
    def _():
        for child in range(1, LEVEL1):
            greet(child, quarter)

    @pl.when(is_first)
    def _():
        for step in range(FIRST - 1):
            greet(1 + lax.rem(me + step, FIRST), quarter)
        repeat(FRONT - LEVEL1, lambda index: greet(LEVEL1 + index, quarter))

    @pl.when(jnp.logical_and(is_first, is_relay))
    def _():
        repeat(CLIQUES - FRONT, lambda index: greet(FRONT + index, quarter))

    @pl.when(jnp.logical_and(jnp.logical_not(is_early), is_relay))
    def _():
        def one(index):
            greet(LEVEL1 + index + (index >= me - LEVEL1).astype(jnp.int32), quarter)

        repeat(CLIQUES - LEVEL1 - 1, one)

    def partial_lse(step):
        base = peer(step) * ROWS

        def one(block):
            rows = pl.ds(pl.multiple_of(base + block * 8, 8), 8)
            slab = pot[:, rows, :]
            largest = jnp.max(slab, axis=0)
            partial[rows, :] = largest + jnp.log(jnp.sum(jnp.exp(slab - largest[None]), axis=0))

        pot_copy(step).wait()
        repeat(ROWS // 8, one, unroll=4)

    partial_lse(1)

    @pl.when(is_root)
    def _():
        pl.semaphore_wait(barrier, peers)

    @pl.when(is_first)
    def _():
        pl.semaphore_wait(barrier, peers + FIRST)
        pl.semaphore_signal(sem_near, inc=1, device_id=(0, quarter), device_id_type=MESH)

    @pl.when(jnp.logical_and(jnp.logical_not(is_early), me < FRONT))
    def _():
        pl.semaphore_wait(barrier, peers + RELAYS - odd + 2)
        for child in range(1, LEVEL1):
            pl.semaphore_signal(sem_far, inc=1, device_id=(child, quarter), device_id_type=MESH)

    @pl.when(me >= FRONT)
    def _():
        pl.semaphore_wait(barrier, peers + RELAYS)

    for step in order:
        if step != order[0]:
            partial_lse(step)
        if step:
            send(partial.at[rows_of(peer(step))], partial_in.at[step - 1], sem_l0, (me, peer(step)))

    for copy in small:
        copy.wait()
    for relay in range(RELAYS):
        sub_measured[relay] = measured[relay * SUB:(relay + 1) * SUB, :]

    def give_measured(relay):
        @pl.when(me != 2 * relay + 1)
        def _():
            send(sub_measured.at[relay], relay_measured.at[me], sem_measured, (2 * relay + 1, quarter))

    @pl.when(jnp.logical_not(is_early))
    def _():
        repeat(RELAYS, give_measured)

    @pl.when(is_inner)
    def _():
        def turn(a0):
            pot_t[a0] = pot[a0].T

        repeat(ROWS, turn, unroll=4)

    def gather_l0():
        await_bytes(partial_in, sem_l0, 1)
        mine = partial[rows_of(quarter), :]
        largest = jnp.maximum(mine, jnp.max(partial_in[...], axis=0))
        summed = jnp.exp(mine - largest) + jnp.sum(jnp.exp(partial_in[...] - largest[None]), axis=0)
        own_l0[...] = largest + jnp.log(summed)

    def share_l0():
        for step in range(1, QUARTERS):
            send(own_l0, whole_l0.at[quarter], sem_whole, (me, peer(step)))
        whole_l0[quarter] = own_l0[...]

    @pl.when(is_root)
    def _():
        message[...] = jnp.zeros_like(message)

    @pl.when(jnp.logical_not(is_root))
    def _():
        gather_l0()
        share_l0()

    @pl.when(is_first)
    def _():
        await_bytes(message, sem_first, 1)

    @pl.when(is_second)
    def _():
        await_bytes(candidates, sem_second, 1)
        message[quarter] = candidates[jnp.maximum(parents[me] - 1, 0)]
        for step in range(1, QUARTERS):
            send(message.at[quarter], message.at[quarter], sem_rows, (me, peer(step)))
        await_bytes(message.at[pl.ds(0, QUARTERS - 1)], sem_rows, 1)

    @pl.when(is_inner)
    def _():
        for other in range(QUARTERS):
            message_t[:, other * ROWS:(other + 1) * ROWS] = message[other].T

        def eight(group):
            rows = pl.ds(pl.multiple_of(group * 8, 8), 8)
            for kind in (1, 2):
                tops, totals = [], []
                for step in range(8):
                    a0 = group * 8 + step
                    if kind == 1:
                        belief = (pot[a0].reshape(QUARTERS, ROWS, K) + message[...]).reshape(K, K)
                    else:
                        belief = pot_t[a0] + message_t[...]
                    largest = jnp.max(belief, axis=0, keepdims=True)
                    tops.append(largest)
                    totals.append(jnp.sum(jnp.exp(belief - largest), axis=0, keepdims=True))
                tables[kind, rows, :] = jnp.concatenate(tops, 0) + jnp.log(jnp.concatenate(totals, 0))

        repeat(ROWS // 8, eight, unroll=2)

    @pl.when(is_root)
    def _():
        gather_l0()

    @pl.when(is_inner)
    def _():
        tables[0] = own_l0[...] + message[quarter]

    @pl.when(is_root)
    def _():
        pl.semaphore_wait(sem_near, FIRST)
        for child in reversed(range(FIRST)):
            to_first[child] = tables[kinds[1 + child]]
            for step in far_first:
                send(to_first.at[child], message.at[quarter], sem_first, (1 + child, peer(step)))
        send(sub_measured, forwarded, sem_forward, (1, quarter))

    @pl.when(is_first)
    def _():
        pl.semaphore_wait(sem_far, FRONT - LEVEL1)

        def give(index):
            child = lax.rem(index + 3, SECOND)
            to_second[child] = tables[kinds[LEVEL1 + child]]
            send(to_second.at[child], candidates.at[me - 1], sem_second, (LEVEL1 + child, quarter))

        repeat(SECOND, give)
        repeat(RELAYS, give_measured)

    @pl.when(me == 1)
    def _():
        await_bytes(forwarded, sem_forward, 1)

        def give(index):
            relay = 1 + index
            send(forwarded.at[relay], relay_measured.at[0], sem_measured, (2 * relay + 1, quarter))

        repeat(RELAYS - 1, give)
        relay_measured[0] = forwarded[0]

    @pl.when(is_second)
    def _():
        slot = me - LEVEL1
        for kind in range(3):
            for relay in range(RELAYS):
                sub_tables[relay, kind] = tables[kind, relay * SUB:(relay + 1) * SUB, :]

        def give_tables(relay):
            @pl.when(me != 2 * relay + 1)
            def _():
                send(sub_tables.at[relay], relay_tables.at[slot], sem_relay, (2 * relay + 1, quarter))

        repeat(RELAYS, give_tables)

    @pl.when(is_root)
    def _():
        share_l0()

    relay_slot = me // 2

    @pl.when(me == 1)
    def _():
        await_bytes(relay_measured.at[pl.ds(0, CLIQUES - 2)], sem_measured, 1)

    @pl.when(jnp.logical_and(is_relay, me != 1))
    def _():
        await_bytes(relay_measured.at[pl.ds(0, CLIQUES - 1)], sem_measured, 1)

    @pl.when(is_relay)
    def _():
        relay_measured[me] = sub_measured[relay_slot]
        clique = lax.broadcasted_iota(jnp.int32, (CLIQUES, CLIQUES), 0)
        chosen = (clique == targets[...]).astype(jnp.float32)
        for row in range(SUB):
            measured_to_leaf[:, row, :] = jnp.dot(
                chosen, relay_measured[:, row, :],
                precision=lax.Precision.HIGHEST, preferred_element_type=jnp.float32,
            )

        def give(leaf):
            child = LEVEL2 + leaf

            @pl.when(child != me)
            def _():
                send(measured_to_leaf.at[child], whole_measured.at[quarter, relay_slot], sem_given, (child, quarter))

        repeat(LEAVES, give)

    @pl.when(jnp.logical_and(is_relay, is_second))
    def _():
        relay_tables[me - LEVEL1] = sub_tables[relay_slot]
        await_bytes(relay_tables.at[pl.ds(0, SECOND - 1)], sem_relay, 1)

    @pl.when(jnp.logical_and(is_relay, jnp.logical_not(is_second)))
    def _():
        await_bytes(relay_tables, sem_relay, 1)

    @pl.when(is_relay)
    def _():
        place = quarter * RELAYS + relay_slot

        def give_leaf(index):
            plane = lax.rem(index, PLANES * 2)
            child = 2 * (index // (PLANES * 2)) + 2 * CHIPS * (PLANES - plane // 2) + lax.rem(index, 2)
            leaf = jnp.maximum(child - LEVEL2, 0)

            @pl.when(child >= LEVEL2)
            def _():
                to_leaf[leaf] = relay_tables[jnp.maximum(parents[child] - LEVEL1, 0), kinds[child]]
                for step in far_first[:-1]:
                    send(to_leaf.at[leaf], from_relay.at[place], sem_leaf, (child, peer(step)))

                @pl.when(child != me)
                def _():
                    send(to_leaf.at[leaf], from_relay.at[place], sem_leaf, (child, quarter))

        repeat(PLANES * CHIPS * 2, give_leaf)

    is_both = jnp.logical_and(is_relay, is_leaf)
    is_plain_leaf = jnp.logical_and(is_leaf, jnp.logical_not(is_relay))

    @pl.when(is_both)
    def _():
        whole_measured[quarter, relay_slot] = measured_to_leaf[me]
        from_relay[quarter * RELAYS + relay_slot] = to_leaf[me - LEVEL2]
        await_bytes(whole_measured.at[0, pl.ds(0, RELAYS - 1)], sem_given, 1)

    @pl.when(is_plain_leaf)
    def _():
        await_bytes(whole_measured.at[0], sem_given, 1)

    await_bytes(whole_l0.at[pl.ds(0, QUARTERS - 1)], sem_whole, 1)

    @pl.when(is_inner)
    def _():
        out[:, 0] = whole_l0[...] + message[...]
        out[:, 1] = jnp.zeros((QUARTERS, ROWS, K), jnp.float32)

    @pl.when(is_leaf)
    def _():
        for step in range(1, QUARTERS):
            send(whole_measured.at[quarter], whole_measured.at[quarter], sem_gather, (me, peer(step)))
        await_bytes(whole_measured.at[pl.ds(0, QUARTERS - 1)], sem_gather, 1)
        for other in range(QUARTERS):
            for relay in range(RELAYS):
                out[other, 1, relay * SUB:(relay + 1) * SUB, :] = whole_measured[other, relay]

    @pl.when(is_both)
    def _():
        await_bytes(from_relay.at[pl.ds(0, CLIQUES - 1)], sem_leaf, 1)

    @pl.when(is_plain_leaf)
    def _():
        await_bytes(from_relay, sem_leaf, 1)

    @pl.when(is_leaf)
    def _():
        for other in range(QUARTERS):
            for relay in range(RELAYS):
                rows = slice(relay * SUB, (relay + 1) * SUB)
                out[other, 0, rows, :] = whole_l0[other, rows, :] + from_relay[other * RELAYS + relay]

    await_bytes(partial_in, sem_l0, 0)
    await_bytes(whole_l0.at[pl.ds(0, QUARTERS - 1)], sem_whole, 0)

    @pl.when(is_root)
    def _():
        await_bytes(sub_measured, sem_forward, 0)
        for _ in range(QUARTERS):
            await_bytes(to_first, sem_first, 0)

    @pl.when(is_first)
    def _():
        await_bytes(to_second, sem_second, 0)

    @pl.when(me == 1)
    def _():
        await_bytes(forwarded.at[pl.ds(0, RELAYS - 1)], sem_measured, 0)

    @pl.when(is_second)
    def _():
        await_bytes(message.at[pl.ds(0, QUARTERS - 1)], sem_rows, 0)

    @pl.when(jnp.logical_and(is_second, is_relay))
    def _():
        await_bytes(sub_tables.at[pl.ds(0, RELAYS - 1)], sem_relay, 0)

    @pl.when(jnp.logical_and(is_second, jnp.logical_not(is_relay)))
    def _():
        await_bytes(sub_tables, sem_relay, 0)

    @pl.when(is_relay)
    def _():
        await_bytes(sub_measured.at[pl.ds(0, RELAYS - 1)], sem_measured, 0)
        for _ in range(QUARTERS - 1):
            await_bytes(to_leaf, sem_leaf, 0)

    @pl.when(is_both)
    def _():
        await_bytes(measured_to_leaf.at[pl.ds(0, LEAVES - 1)], sem_given, 0)
        await_bytes(to_leaf.at[pl.ds(0, LEAVES - 1)], sem_leaf, 0)

    @pl.when(jnp.logical_and(is_relay, is_inner))
    def _():
        await_bytes(measured_to_leaf.at[pl.ds(0, LEAVES)], sem_given, 0)
        await_bytes(to_leaf, sem_leaf, 0)

    @pl.when(is_leaf)
    def _():
        await_bytes(whole_measured.at[pl.ds(0, QUARTERS - 1)], sem_gather, 0)

    @pl.when(jnp.logical_not(jnp.logical_or(is_root, is_relay)))
    def _():
        await_bytes(sub_measured, sem_measured, 0)


def sweep(parents, kinds, targets, pot, measured):
    hbm, vmem = pl.BlockSpec(memory_space=pltpu.HBM), pl.BlockSpec(memory_space=pltpu.VMEM)
    f32 = jnp.float32
    scratch = [
        (ROWS, K),
        (K, K), (QUARTERS - 1, ROWS, K), (ROWS, K), (QUARTERS, ROWS, K), (QUARTERS, ROWS, K), (K, K), (ROWS, K, K),
        (3, ROWS, K),
        (FIRST, ROWS, K), (SECOND, ROWS, K), (FIRST, ROWS, K), (RELAYS, 3, SUB, K), (SECOND, 3, SUB, K),
        (RELAYS, SUB, K), (RELAYS, SUB, K), (CLIQUES, SUB, K), (CLIQUES, SUB, K), (QUARTERS, RELAYS, SUB, K),
        (LEAVES, SUB, K), (QUARTERS * RELAYS, SUB, K),
    ]
    return pl.pallas_call(
        sweep_kernel,
        out_shape=(
            jax.ShapeDtypeStruct((QUARTERS, 2, ROWS, K), f32),
            jax.ShapeDtypeStruct((ROWS, K, K), f32),
        ),
        in_specs=[hbm] * 5,
        out_specs=(vmem, vmem),
        scratch_shapes=[
            pltpu.SMEM((CLIQUES,), jnp.int32), pltpu.SMEM((CLIQUES,), jnp.int32), pltpu.VMEM((1, CLIQUES), jnp.int32),
            *(pltpu.VMEM(shape, f32) for shape in scratch),
            pltpu.SemaphoreType.DMA((4,)), pltpu.SemaphoreType.DMA((QUARTERS,)),
            *[pltpu.SemaphoreType.DMA((2,))] * 11,
            pltpu.SemaphoreType.REGULAR, pltpu.SemaphoreType.REGULAR,
        ],
        compiler_params=pltpu.CompilerParams(
            collective_id=0, has_side_effects=True, vmem_limit_bytes=16 * 1024 * 1024
        ),
        name="sweep",
    )(parents, kinds, targets, pot, measured)


BLOCK = 8


def finish_kernel(final, pot, marginal_hbm, updated_hbm, marginal, updated, sem):
    me = lax.axis_index("wide")
    quarter = lax.axis_index("narrow")
    cells = final[:, 0]
    largest = jnp.max(cells)
    weights = jnp.exp(cells - largest)
    scale = jnp.float32(K * K) / jnp.sum(weights)
    whole = weights * scale
    marginal[...] = jnp.exp(final[quarter, 0] - largest) * scale
    copies = [pltpu.make_async_copy(marginal, marginal_hbm, sem.at[0])]
    copies[0].start()
    term = jnp.where(me >= LEVEL2, jnp.float32(0.5) * (whole - final[:, 1]), jnp.float32(0.0)).reshape(K, K)
    for block in range(ROWS // BLOCK):
        rows = slice(block * BLOCK, (block + 1) * BLOCK)
        updated[rows] = pot[rows] - term[None]
        copies.append(pltpu.make_async_copy(updated.at[rows], updated_hbm.at[rows], sem.at[1 + block]))
        copies[-1].start()
    for copy in copies:
        copy.wait()


def finish(final, pot):
    hbm, vmem = pl.BlockSpec(memory_space=pltpu.HBM), pl.BlockSpec(memory_space=pltpu.VMEM)
    shapes = (ROWS, K), (ROWS, K, K)
    return pl.pallas_call(
        finish_kernel,
        out_shape=tuple(jax.ShapeDtypeStruct(shape, jnp.float32) for shape in shapes),
        in_specs=[vmem, vmem],
        out_specs=(hbm, hbm),
        scratch_shapes=[*(pltpu.VMEM(shape, jnp.float32) for shape in shapes), pltpu.SemaphoreType.DMA((1 + ROWS // BLOCK,))],
        compiler_params=pltpu.CompilerParams(vmem_limit_bytes=16 * 1024 * 1024),
        name="finish",
    )(final, pot)


def body(potentials, parents, separator_excluded, measurement_clique, measured):
    parents, separator_excluded, measurement_clique, measured, potentials = (
        pltpu.with_memory_space_constraint(array, pltpu.HBM)
        for array in (parents, separator_excluded, measurement_clique[None], measured[0], potentials[0])
    )
    pot = potentials
    final, pot = sweep(parents, separator_excluded, measurement_clique, pot, measured)
    marginal, updated = finish(final, pot)
    return marginal[None], updated[None]


def solution(mesh):
    return jax.shard_map(
        body,
        mesh=mesh,
        in_specs=(P("wide", "narrow", None, None), P(), P(), P(), P("wide", "narrow", None)),
        out_specs=(P("wide", "narrow", None), P("wide", "narrow", None, None)),
        check_vma=False,
    )
```

```python
import functools

import jax
import jax.numpy as jnp
from jax import lax
from jax.experimental import pallas as pl
from jax.experimental.pallas import tpu as pltpu
from jax.sharding import PartitionSpec as P

MESH = pl.DeviceIdType.MESH
K = 128
QUARTERS = 4
ROWS = K // QUARTERS
CLIQUES = 64
LEVEL1, LEVEL2 = 5, 21
FIRST = LEVEL1 - 1
SECOND = LEVEL2 - LEVEL1
LEAVES = CLIQUES - LEVEL2
RELAYS = 16
SUB = ROWS // RELAYS
CHIPS, PLANES = 8, 3


FARTHEST = (5, 7, 6, 8, 11, 3, 9, 12, 4, 10, 13, 1, 14, 2, 15, 0)


SERVE = (0, 1, 2, 6, 5, 3, 7, 4)


def sweep_kernel(
    parents_hbm, kinds_hbm, targets_hbm, pot_hbm, measured_hbm, out, pot,
    parents, kinds, targets, measured,
    partial, partial_in, own_l0, whole_l0, message, message_t, pot_t, tables,
    to_first, to_second, candidates, sub_tables, relay_tables,
    sub_measured, forwarded, relay_measured, measured_to_leaf, whole_measured, to_leaf, from_relay,
    sem_small, sem_pot,
    sem_l0, sem_whole, sem_first, sem_second, sem_rows, sem_relay, sem_forward, sem_measured, sem_given, sem_gather, sem_leaf,
    sem_near, sem_far,
):
    me = lax.axis_index("wide")
    quarter = lax.axis_index("narrow")
    is_root = me == 0
    is_first = jnp.logical_and(me >= 1, me < LEVEL1)
    is_second = jnp.logical_and(me >= LEVEL1, me < LEVEL2)
    is_leaf = me >= LEVEL2
    is_inner = me < LEVEL2
    odd = lax.rem(me, 2)
    is_relay = jnp.logical_and(odd == 1, lax.rem(me, 2 * CHIPS) < CHIPS)
    is_early = me < LEVEL1
    peers = QUARTERS - 1

    def peer(step):
        return lax.rem(quarter + step, QUARTERS)

    def relay_device(relay):
        return 2 * CHIPS * (relay // (CHIPS // 2)) + 2 * lax.rem(relay, CHIPS // 2) + 1

    def rows_of(part):
        return pl.ds(pl.multiple_of(part * ROWS, ROWS), ROWS)

    def repeat(count, function, unroll=1):
        def run(index, carry):
            function(index)
            return carry

        lax.fori_loop(0, count, run, 0, unroll=unroll)

    def send(source, target, sem, device):
        pltpu.make_async_remote_copy(
            src_ref=source, dst_ref=target, send_sem=sem.at[0], recv_sem=sem.at[1],
            device_id=device, device_id_type=MESH,
        ).start()

    def await_bytes(like, sem, which):
        pltpu.make_async_copy(like, like, sem.at[which]).wait()

    small = [
        pltpu.make_async_copy(source, target, sem_small.at[index])
        for index, (source, target) in enumerate(
            ((parents_hbm, parents), (kinds_hbm, kinds), (targets_hbm, targets), (measured_hbm, measured))
        )
    ]

    def pot_copy(step):
        rows = rows_of(peer(step))
        return pltpu.make_async_copy(pot_hbm.at[:, rows], pot.at[:, rows], sem_pot.at[step])

    far_first = (2, 1, 3, 0)
    order = far_first
    for step in order:
        pot_copy(step).start()
    for copy in small:
        copy.start()

    barrier = pltpu.get_barrier_semaphore()

    def greet(wide, narrow):
        pl.semaphore_signal(barrier, inc=1, device_id=(wide, narrow), device_id_type=MESH)

    for step in range(1, QUARTERS):
        greet(me, peer(step))

    @pl.when(is_root)
    def _():
        for child in range(1, LEVEL1):
            greet(child, quarter)

    @pl.when(is_first)
    def _():
        for step in range(FIRST - 1):
            greet(1 + lax.rem(me + step, FIRST), quarter)
        repeat(CLIQUES - LEVEL1, lambda index: greet(LEVEL1 + index, quarter))

    @pl.when(jnp.logical_and(jnp.logical_not(is_early), is_relay))
    def _():
        def one(index):
            greet(LEVEL1 + index + (index >= me - LEVEL1).astype(jnp.int32), quarter)

        repeat(CLIQUES - LEVEL1 - 1, one)

    def partial_lse(step):
        base = peer(step) * ROWS

        def one(block):
            rows = pl.ds(pl.multiple_of(base + block * 8, 8), 8)
            slab = pot[:, rows, :]
            largest = jnp.max(slab, axis=0)
            partial[rows, :] = largest + jnp.log(jnp.sum(jnp.exp(slab - largest[None]), axis=0))

        pot_copy(step).wait()
        repeat(ROWS // 8, one, unroll=4)

    partial_lse(order[0])

    @pl.when(is_root)
    def _():
        pl.semaphore_wait(barrier, peers)

    @pl.when(is_first)
    def _():
        pl.semaphore_wait(barrier, peers + FIRST)
        pl.semaphore_signal(sem_near, inc=1, device_id=(0, quarter), device_id_type=MESH)

    @pl.when(jnp.logical_not(is_early))
    def _():
        pl.semaphore_wait(barrier, peers + RELAYS - is_relay.astype(jnp.int32) + 2)

    @pl.when(jnp.logical_or(is_second, jnp.logical_and(is_relay, is_leaf)))
    def _():
        for child in range(1, LEVEL1):
            pl.semaphore_signal(sem_far, inc=1, device_id=(child, quarter), device_id_type=MESH)

    for step in order:
        if step != order[0]:
            partial_lse(step)
        if step:
            send(partial.at[rows_of(peer(step))], partial_in.at[step - 1], sem_l0, (me, peer(step)))

    for copy in small:
        copy.wait()
    for relay in range(RELAYS):
        sub_measured[relay] = measured[relay * SUB:(relay + 1) * SUB, :]

    def give_measured(relay):
        @pl.when(me != relay_device(relay))
        def _():
            send(sub_measured.at[relay], relay_measured.at[me], sem_measured, (relay_device(relay), quarter))

    @pl.when(jnp.logical_not(is_early))
    def _():
        repeat(RELAYS, give_measured)

    @pl.when(is_inner)
    def _():
        def turn(a0):
            pot_t[a0] = pot[a0].T

        repeat(ROWS, turn, unroll=4)

    def gather_l0():
        await_bytes(partial_in, sem_l0, 1)
        mine = partial[rows_of(quarter), :]
        largest = jnp.maximum(mine, jnp.max(partial_in[...], axis=0))
        summed = jnp.exp(mine - largest) + jnp.sum(jnp.exp(partial_in[...] - largest[None]), axis=0)
        own_l0[...] = largest + jnp.log(summed)

    def share_l0():
        for step in range(1, QUARTERS):
            send(own_l0, whole_l0.at[quarter], sem_whole, (me, peer(step)))
        whole_l0[quarter] = own_l0[...]

    @pl.when(is_root)
    def _():
        message[...] = jnp.zeros_like(message)

    @pl.when(jnp.logical_not(is_root))
    def _():
        gather_l0()
        share_l0()

    @pl.when(is_first)
    def _():
        await_bytes(message, sem_first, 1)

    @pl.when(is_second)
    def _():
        await_bytes(candidates, sem_second, 1)
        message[quarter] = candidates[jnp.maximum(parents[me] - 1, 0)]
        for step in far_first[:-1]:
            send(message.at[quarter], message.at[quarter], sem_rows, (me, peer(step)))
        await_bytes(message.at[pl.ds(0, QUARTERS - 1)], sem_rows, 1)

    @pl.when(is_inner)
    def _():
        for other in range(QUARTERS):
            message_t[:, other * ROWS:(other + 1) * ROWS] = message[other].T

        def eight(group):
            rows = pl.ds(pl.multiple_of(group * 8, 8), 8)
            for kind in (1, 2):
                tops, totals = [], []
                for step in range(8):
                    a0 = group * 8 + step
                    if kind == 1:
                        belief = (pot[a0].reshape(QUARTERS, ROWS, K) + message[...]).reshape(K, K)
                    else:
                        belief = pot_t[a0] + message_t[...]
                    largest = jnp.max(belief, axis=0, keepdims=True)
                    tops.append(largest)
                    totals.append(jnp.sum(jnp.exp(belief - largest), axis=0, keepdims=True))
                tables[kind, rows, :] = jnp.concatenate(tops, 0) + jnp.log(jnp.concatenate(totals, 0))

        repeat(ROWS // 8, eight, unroll=2)

    @pl.when(is_root)
    def _():
        gather_l0()

    @pl.when(is_inner)
    def _():
        tables[0] = own_l0[...] + message[quarter]

    @pl.when(is_root)
    def _():
        pl.semaphore_wait(sem_near, FIRST)
        for child in reversed(range(FIRST)):
            to_first[child] = tables[kinds[1 + child]]
            for step in far_first:
                send(to_first.at[child], message.at[quarter], sem_first, (1 + child, peer(step)))
        send(sub_measured, forwarded, sem_forward, (1, quarter))

    @pl.when(is_first)
    def _():
        pl.semaphore_wait(sem_far, SECOND + 10)

        for child in FARTHEST:
            to_second[child] = tables[kinds[LEVEL1 + child]]
            send(to_second.at[child], candidates.at[me - 1], sem_second, (LEVEL1 + child, quarter))

        repeat(RELAYS, give_measured)

    @pl.when(me == 1)
    def _():
        await_bytes(forwarded, sem_forward, 1)

        def give(index):
            relay = 1 + index
            send(forwarded.at[relay], relay_measured.at[0], sem_measured, (relay_device(relay), quarter))

        repeat(RELAYS - 1, give)
        relay_measured[0] = forwarded[0]

    @pl.when(is_second)
    def _():
        slot = me - LEVEL1
        for kind in range(3):
            for relay in range(RELAYS):
                sub_tables[relay, kind] = tables[kind, relay * SUB:(relay + 1) * SUB, :]

        def give_tables(relay):
            @pl.when(me != relay_device(relay))
            def _():
                send(sub_tables.at[relay], relay_tables.at[slot], sem_relay, (relay_device(relay), quarter))

        repeat(RELAYS, give_tables)

    @pl.when(is_root)
    def _():
        share_l0()

    relay_slot = (CHIPS // 2) * (me // (2 * CHIPS)) + lax.rem(me, 2 * CHIPS) // 2

    @pl.when(me == 1)
    def _():
        await_bytes(relay_measured.at[pl.ds(0, CLIQUES - 2)], sem_measured, 1)

    @pl.when(jnp.logical_and(is_relay, me != 1))
    def _():
        await_bytes(relay_measured.at[pl.ds(0, CLIQUES - 1)], sem_measured, 1)

    @pl.when(is_relay)
    def _():
        relay_measured[me] = sub_measured[relay_slot]
        clique = lax.broadcasted_iota(jnp.int32, (CLIQUES, CLIQUES), 0)
        chosen = (clique == targets[...]).astype(jnp.float32)
        for row in range(SUB):
            measured_to_leaf[:, row, :] = jnp.dot(
                chosen, relay_measured[:, row, :],
                precision=lax.Precision.HIGHEST, preferred_element_type=jnp.float32,
            )

        def give(leaf):
            child = LEVEL2 + leaf

            @pl.when(child != me)
            def _():
                send(measured_to_leaf.at[child], whole_measured.at[quarter, relay_slot], sem_given, (child, quarter))

        repeat(LEAVES, give)

    @pl.when(jnp.logical_and(is_relay, is_second))
    def _():
        relay_tables[me - LEVEL1] = sub_tables[relay_slot]
        await_bytes(relay_tables.at[pl.ds(0, SECOND - 1)], sem_relay, 1)

    @pl.when(jnp.logical_and(is_relay, jnp.logical_not(is_second)))
    def _():
        await_bytes(relay_tables, sem_relay, 1)

    @pl.when(is_relay)
    def _():
        place = quarter * RELAYS + relay_slot

        def give_leaf(chip, plane):
            child = 2 * chip + 2 * CHIPS * (PLANES - plane // 2) + lax.rem(plane, 2)
            leaf = jnp.maximum(child - LEVEL2, 0)

            @pl.when(child >= LEVEL2)
            def _():
                to_leaf[leaf] = relay_tables[jnp.maximum(parents[child] - LEVEL1, 0), kinds[child]]
                for step in far_first[:-1]:
                    send(to_leaf.at[leaf], from_relay.at[place], sem_leaf, (child, peer(step)))

                @pl.when(child != me)
                def _():
                    send(to_leaf.at[leaf], from_relay.at[place], sem_leaf, (child, quarter))

        for chip in SERVE:
            repeat(PLANES * 2, functools.partial(give_leaf, chip))

    is_both = jnp.logical_and(is_relay, is_leaf)
    is_plain_leaf = jnp.logical_and(is_leaf, jnp.logical_not(is_relay))

    @pl.when(is_both)
    def _():
        whole_measured[quarter, relay_slot] = measured_to_leaf[me]
        from_relay[quarter * RELAYS + relay_slot] = to_leaf[me - LEVEL2]
        await_bytes(whole_measured.at[0, pl.ds(0, RELAYS - 1)], sem_given, 1)

    @pl.when(is_plain_leaf)
    def _():
        await_bytes(whole_measured.at[0], sem_given, 1)

    await_bytes(whole_l0.at[pl.ds(0, QUARTERS - 1)], sem_whole, 1)

    @pl.when(is_inner)
    def _():
        out[:, 0] = whole_l0[...] + message[...]
        out[:, 1] = jnp.zeros((QUARTERS, ROWS, K), jnp.float32)

    @pl.when(is_leaf)
    def _():
        for step in range(1, QUARTERS):
            send(whole_measured.at[quarter], whole_measured.at[quarter], sem_gather, (me, peer(step)))
        await_bytes(whole_measured.at[pl.ds(0, QUARTERS - 1)], sem_gather, 1)
        for other in range(QUARTERS):
            for relay in range(RELAYS):
                out[other, 1, relay * SUB:(relay + 1) * SUB, :] = whole_measured[other, relay]

    @pl.when(is_both)
    def _():
        await_bytes(from_relay.at[pl.ds(0, CLIQUES - 1)], sem_leaf, 1)

    @pl.when(is_plain_leaf)
    def _():
        await_bytes(from_relay, sem_leaf, 1)

    @pl.when(is_leaf)
    def _():
        for other in range(QUARTERS):
            for relay in range(RELAYS):
                rows = slice(relay * SUB, (relay + 1) * SUB)
                out[other, 0, rows, :] = whole_l0[other, rows, :] + from_relay[other * RELAYS + relay]

    await_bytes(partial_in, sem_l0, 0)
    await_bytes(whole_l0.at[pl.ds(0, QUARTERS - 1)], sem_whole, 0)

    @pl.when(is_root)
    def _():
        await_bytes(sub_measured, sem_forward, 0)
        for _ in range(QUARTERS):
            await_bytes(to_first, sem_first, 0)

    @pl.when(is_first)
    def _():
        await_bytes(to_second, sem_second, 0)

    @pl.when(me == 1)
    def _():
        await_bytes(forwarded.at[pl.ds(0, RELAYS - 1)], sem_measured, 0)

    @pl.when(is_second)
    def _():
        await_bytes(message.at[pl.ds(0, QUARTERS - 1)], sem_rows, 0)

    @pl.when(jnp.logical_and(is_second, is_relay))
    def _():
        await_bytes(sub_tables.at[pl.ds(0, RELAYS - 1)], sem_relay, 0)

    @pl.when(jnp.logical_and(is_second, jnp.logical_not(is_relay)))
    def _():
        await_bytes(sub_tables, sem_relay, 0)

    @pl.when(is_relay)
    def _():
        await_bytes(sub_measured.at[pl.ds(0, RELAYS - 1)], sem_measured, 0)
        for _ in range(QUARTERS - 1):
            await_bytes(to_leaf, sem_leaf, 0)

    @pl.when(is_both)
    def _():
        await_bytes(measured_to_leaf.at[pl.ds(0, LEAVES - 1)], sem_given, 0)
        await_bytes(to_leaf.at[pl.ds(0, LEAVES - 1)], sem_leaf, 0)

    @pl.when(jnp.logical_and(is_relay, is_inner))
    def _():
        await_bytes(measured_to_leaf.at[pl.ds(0, LEAVES)], sem_given, 0)
        await_bytes(to_leaf, sem_leaf, 0)

    @pl.when(is_leaf)
    def _():
        await_bytes(whole_measured.at[pl.ds(0, QUARTERS - 1)], sem_gather, 0)

    @pl.when(jnp.logical_not(jnp.logical_or(is_root, is_relay)))
    def _():
        await_bytes(sub_measured, sem_measured, 0)


def sweep(parents, kinds, targets, pot, measured):
    hbm, vmem = pl.BlockSpec(memory_space=pltpu.HBM), pl.BlockSpec(memory_space=pltpu.VMEM)
    f32 = jnp.float32
    scratch = [
        (ROWS, K),
        (K, K), (QUARTERS - 1, ROWS, K), (ROWS, K), (QUARTERS, ROWS, K), (QUARTERS, ROWS, K), (K, K), (ROWS, K, K),
        (3, ROWS, K),
        (FIRST, ROWS, K), (SECOND, ROWS, K), (FIRST, ROWS, K), (RELAYS, 3, SUB, K), (SECOND, 3, SUB, K),
        (RELAYS, SUB, K), (RELAYS, SUB, K), (CLIQUES, SUB, K), (CLIQUES, SUB, K), (QUARTERS, RELAYS, SUB, K),
        (LEAVES, SUB, K), (QUARTERS * RELAYS, SUB, K),
    ]
    return pl.pallas_call(
        sweep_kernel,
        out_shape=(
            jax.ShapeDtypeStruct((QUARTERS, 2, ROWS, K), f32),
            jax.ShapeDtypeStruct((ROWS, K, K), f32),
        ),
        in_specs=[hbm] * 5,
        out_specs=(vmem, vmem),
        scratch_shapes=[
            pltpu.SMEM((CLIQUES,), jnp.int32), pltpu.SMEM((CLIQUES,), jnp.int32), pltpu.VMEM((1, CLIQUES), jnp.int32),
            *(pltpu.VMEM(shape, f32) for shape in scratch),
            pltpu.SemaphoreType.DMA((4,)), pltpu.SemaphoreType.DMA((QUARTERS,)),
            *[pltpu.SemaphoreType.DMA((2,))] * 11,
            pltpu.SemaphoreType.REGULAR, pltpu.SemaphoreType.REGULAR,
        ],
        compiler_params=pltpu.CompilerParams(
            collective_id=0, has_side_effects=True, vmem_limit_bytes=16 * 1024 * 1024
        ),
        name="sweep",
    )(parents, kinds, targets, pot, measured)


BLOCK = 8


def finish_kernel(final, pot, marginal_hbm, updated_hbm, marginal, updated, sem):
    me = lax.axis_index("wide")
    quarter = lax.axis_index("narrow")
    cells = final[:, 0]
    largest = jnp.max(cells)
    weights = jnp.exp(cells - largest)
    scale = jnp.float32(K * K) / jnp.sum(weights)
    whole = weights * scale
    marginal[...] = jnp.exp(final[quarter, 0] - largest) * scale
    copies = [pltpu.make_async_copy(marginal, marginal_hbm, sem.at[0])]
    copies[0].start()
    term = jnp.where(me >= LEVEL2, jnp.float32(0.5) * (whole - final[:, 1]), jnp.float32(0.0)).reshape(K, K)
    for block in range(ROWS // BLOCK):
        rows = slice(block * BLOCK, (block + 1) * BLOCK)
        updated[rows] = pot[rows] - term[None]
        copies.append(pltpu.make_async_copy(updated.at[rows], updated_hbm.at[rows], sem.at[1 + block]))
        copies[-1].start()
    for copy in copies:
        copy.wait()


def finish(final, pot):
    hbm, vmem = pl.BlockSpec(memory_space=pltpu.HBM), pl.BlockSpec(memory_space=pltpu.VMEM)
    shapes = (ROWS, K), (ROWS, K, K)
    return pl.pallas_call(
        finish_kernel,
        out_shape=tuple(jax.ShapeDtypeStruct(shape, jnp.float32) for shape in shapes),
        in_specs=[vmem, vmem],
        out_specs=(hbm, hbm),
        scratch_shapes=[*(pltpu.VMEM(shape, jnp.float32) for shape in shapes), pltpu.SemaphoreType.DMA((1 + ROWS // BLOCK,))],
        compiler_params=pltpu.CompilerParams(vmem_limit_bytes=16 * 1024 * 1024),
        name="finish",
    )(final, pot)


def body(potentials, parents, separator_excluded, measurement_clique, measured):
    parents, separator_excluded, measurement_clique, measured, potentials = (
        pltpu.with_memory_space_constraint(array, pltpu.HBM)
        for array in (parents, separator_excluded, measurement_clique[None], measured[0], potentials[0])
    )
    pot = potentials
    final, pot = sweep(parents, separator_excluded, measurement_clique, pot, measured)
    marginal, updated = finish(final, pot)
    return marginal[None], updated[None]


def solution(mesh):
    return jax.shard_map(
        body,
        mesh=mesh,
        in_specs=(P("wide", "narrow", None, None), P(), P(), P(), P("wide", "narrow", None)),
        out_specs=(P("wide", "narrow", None), P("wide", "narrow", None, None)),
        check_vma=False,
    )
```

```python
import functools

import jax
import jax.numpy as jnp
from jax import lax
from jax.experimental import pallas as pl
from jax.experimental.pallas import tpu as pltpu
from jax.sharding import PartitionSpec as P

MESH = pl.DeviceIdType.MESH
K = 128
QUARTERS = 4
ROWS = K // QUARTERS
CLIQUES = 64
LEVEL1, LEVEL2 = 5, 21
FIRST = LEVEL1 - 1
SECOND = LEVEL2 - LEVEL1
LEAVES = CLIQUES - LEVEL2
RELAYS = 16
SUB = ROWS // RELAYS
CHIPS, PLANES = 8, 3


FARTHEST = (5, 7, 6, 8, 11, 3, 9, 12, 4, 10, 13, 1, 14, 2, 15, 0)


SERVE = (0, 1, 2, 3, 6, 5, 4, 7)


def sweep_kernel(
    parents_hbm, kinds_hbm, targets_hbm, pot_hbm, measured_hbm, out, pot,
    parents, kinds, targets, measured,
    partial, partial_in, own_l0, whole_l0, message, message_t, pot_t, tables,
    to_first, to_second, candidates, sub_tables, relay_tables,
    sub_measured, forwarded, relay_measured, measured_to_leaf, whole_measured, to_leaf, from_relay,
    sem_small, sem_pot,
    sem_l0, sem_whole, sem_first, sem_second, sem_rows, sem_relay, sem_forward, sem_measured, sem_given, sem_gather, sem_leaf,
    sem_near, sem_far,
):
    me = lax.axis_index("wide")
    quarter = lax.axis_index("narrow")
    is_root = me == 0
    is_first = jnp.logical_and(me >= 1, me < LEVEL1)
    is_second = jnp.logical_and(me >= LEVEL1, me < LEVEL2)
    is_leaf = me >= LEVEL2
    is_inner = me < LEVEL2
    odd = lax.rem(me, 2)
    is_relay = jnp.logical_and(odd == 1, lax.rem(me, 2 * CHIPS) < CHIPS)
    is_early = me < LEVEL1
    peers = QUARTERS - 1

    def peer(step):
        return lax.rem(quarter + step, QUARTERS)

    def relay_device(relay):
        return 2 * CHIPS * (relay // (CHIPS // 2)) + 2 * lax.rem(relay, CHIPS // 2) + 1

    def rows_of(part):
        return pl.ds(pl.multiple_of(part * ROWS, ROWS), ROWS)

    def repeat(count, function, unroll=1):
        def run(index, carry):
            function(index)
            return carry

        lax.fori_loop(0, count, run, 0, unroll=unroll)

    def send(source, target, sem, device):
        pltpu.make_async_remote_copy(
            src_ref=source, dst_ref=target, send_sem=sem.at[0], recv_sem=sem.at[1],
            device_id=device, device_id_type=MESH,
        ).start()

    def await_bytes(like, sem, which):
        pltpu.make_async_copy(like, like, sem.at[which]).wait()

    small = [
        pltpu.make_async_copy(source, target, sem_small.at[index])
        for index, (source, target) in enumerate(
            ((parents_hbm, parents), (kinds_hbm, kinds), (targets_hbm, targets), (measured_hbm, measured))
        )
    ]

    def pot_copy(step):
        rows = rows_of(peer(step))
        return pltpu.make_async_copy(pot_hbm.at[:, rows], pot.at[:, rows], sem_pot.at[step])

    far_first = (2, 1, 3, 0)
    order = far_first
    for step in order:
        pot_copy(step).start()
    for copy in small:
        copy.start()

    barrier = pltpu.get_barrier_semaphore()

    def greet(wide, narrow):
        pl.semaphore_signal(barrier, inc=1, device_id=(wide, narrow), device_id_type=MESH)

    for step in range(1, QUARTERS):
        greet(me, peer(step))

    @pl.when(is_root)
    def _():
        for child in range(1, LEVEL1):
            greet(child, quarter)

    @pl.when(is_first)
    def _():
        for step in range(FIRST - 1):
            greet(1 + lax.rem(me + step, FIRST), quarter)
        repeat(CLIQUES - LEVEL1, lambda index: greet(LEVEL1 + index, quarter))

    @pl.when(jnp.logical_and(jnp.logical_not(is_early), is_relay))
    def _():
        def one(index):
            greet(LEVEL1 + index + (index >= me - LEVEL1).astype(jnp.int32), quarter)

        repeat(CLIQUES - LEVEL1 - 1, one)

    def partial_lse(step):
        base = peer(step) * ROWS

        def one(block):
            rows = pl.ds(pl.multiple_of(base + block * 8, 8), 8)
            slab = pot[:, rows, :]
            largest = jnp.max(slab, axis=0)
            partial[rows, :] = largest + jnp.log(jnp.sum(jnp.exp(slab - largest[None]), axis=0))

        pot_copy(step).wait()
        repeat(ROWS // 8, one, unroll=4)

    partial_lse(order[0])

    @pl.when(is_root)
    def _():
        pl.semaphore_wait(barrier, peers)

    @pl.when(is_first)
    def _():
        pl.semaphore_wait(barrier, peers + FIRST)
        pl.semaphore_signal(sem_near, inc=1, device_id=(0, quarter), device_id_type=MESH)

    @pl.when(jnp.logical_not(is_early))
    def _():
        pl.semaphore_wait(barrier, peers + RELAYS - is_relay.astype(jnp.int32) + 2)

    @pl.when(jnp.logical_or(is_second, jnp.logical_and(is_relay, is_leaf)))
    def _():
        for child in range(1, LEVEL1):
            pl.semaphore_signal(sem_far, inc=1, device_id=(child, quarter), device_id_type=MESH)

    for step in order:
        if step != order[0]:
            partial_lse(step)
        if step:
            send(partial.at[rows_of(peer(step))], partial_in.at[step - 1], sem_l0, (me, peer(step)))

    for copy in small:
        copy.wait()
    for relay in range(RELAYS):
        sub_measured[relay] = measured[relay * SUB:(relay + 1) * SUB, :]

    def give_measured(relay):
        @pl.when(me != relay_device(relay))
        def _():
            send(sub_measured.at[relay], relay_measured.at[me], sem_measured, (relay_device(relay), quarter))

    @pl.when(jnp.logical_not(is_early))
    def _():
        repeat(RELAYS, give_measured)

    @pl.when(is_inner)
    def _():
        def turn(a0):
            pot_t[a0] = pot[a0].T

        repeat(ROWS, turn, unroll=4)

    def gather_l0():
        await_bytes(partial_in, sem_l0, 1)
        mine = partial[rows_of(quarter), :]
        largest = jnp.maximum(mine, jnp.max(partial_in[...], axis=0))
        summed = jnp.exp(mine - largest) + jnp.sum(jnp.exp(partial_in[...] - largest[None]), axis=0)
        own_l0[...] = largest + jnp.log(summed)

    def share_l0():
        for step in range(1, QUARTERS):
            send(own_l0, whole_l0.at[quarter], sem_whole, (me, peer(step)))
        whole_l0[quarter] = own_l0[...]

    @pl.when(is_root)
    def _():
        message[...] = jnp.zeros_like(message)

    @pl.when(jnp.logical_not(is_root))
    def _():
        gather_l0()
        share_l0()

    @pl.when(is_first)
    def _():
        await_bytes(message, sem_first, 1)

    @pl.when(is_second)
    def _():
        await_bytes(candidates, sem_second, 1)
        message[quarter] = candidates[jnp.maximum(parents[me] - 1, 0)]
        for step in far_first[:-1]:
            send(message.at[quarter], message.at[quarter], sem_rows, (me, peer(step)))
        await_bytes(message.at[pl.ds(0, QUARTERS - 1)], sem_rows, 1)

    @pl.when(is_inner)
    def _():
        for other in range(QUARTERS):
            message_t[:, other * ROWS:(other + 1) * ROWS] = message[other].T

        def eight(group):
            rows = pl.ds(pl.multiple_of(group * 8, 8), 8)
            for kind in (1, 2):
                tops, totals = [], []
                for step in range(8):
                    a0 = group * 8 + step
                    if kind == 1:
                        belief = (pot[a0].reshape(QUARTERS, ROWS, K) + message[...]).reshape(K, K)
                    else:
                        belief = pot_t[a0] + message_t[...]
                    largest = jnp.max(belief, axis=0, keepdims=True)
                    tops.append(largest)
                    totals.append(jnp.sum(jnp.exp(belief - largest), axis=0, keepdims=True))
                tables[kind, rows, :] = jnp.concatenate(tops, 0) + jnp.log(jnp.concatenate(totals, 0))

        repeat(ROWS // 8, eight, unroll=2)

    @pl.when(is_root)
    def _():
        gather_l0()

    @pl.when(is_inner)
    def _():
        tables[0] = own_l0[...] + message[quarter]

    @pl.when(is_root)
    def _():
        pl.semaphore_wait(sem_near, FIRST)
        for child in reversed(range(FIRST)):
            to_first[child] = tables[kinds[1 + child]]
            for step in far_first:
                send(to_first.at[child], message.at[quarter], sem_first, (1 + child, peer(step)))
        send(sub_measured, forwarded, sem_forward, (1, quarter))

    @pl.when(is_first)
    def _():
        pl.semaphore_wait(sem_far, SECOND + 10)

        for child in FARTHEST:
            to_second[child] = tables[kinds[LEVEL1 + child]]
            send(to_second.at[child], candidates.at[me - 1], sem_second, (LEVEL1 + child, quarter))

        repeat(RELAYS, give_measured)

    @pl.when(me == 1)
    def _():
        await_bytes(forwarded, sem_forward, 1)

        def give(index):
            relay = 1 + index
            send(forwarded.at[relay], relay_measured.at[0], sem_measured, (relay_device(relay), quarter))

        repeat(RELAYS - 1, give)
        relay_measured[0] = forwarded[0]

    @pl.when(is_second)
    def _():
        slot = me - LEVEL1
        for kind in range(3):
            for relay in range(RELAYS):
                sub_tables[relay, kind] = tables[kind, relay * SUB:(relay + 1) * SUB, :]

        def give_tables(relay):
            @pl.when(me != relay_device(relay))
            def _():
                send(sub_tables.at[relay], relay_tables.at[slot], sem_relay, (relay_device(relay), quarter))

        repeat(RELAYS, give_tables)

    @pl.when(is_root)
    def _():
        share_l0()

    relay_slot = (CHIPS // 2) * (me // (2 * CHIPS)) + lax.rem(me, 2 * CHIPS) // 2

    @pl.when(me == 1)
    def _():
        await_bytes(relay_measured.at[pl.ds(0, CLIQUES - 2)], sem_measured, 1)

    @pl.when(jnp.logical_and(is_relay, me != 1))
    def _():
        await_bytes(relay_measured.at[pl.ds(0, CLIQUES - 1)], sem_measured, 1)

    @pl.when(is_relay)
    def _():
        relay_measured[me] = sub_measured[relay_slot]
        clique = lax.broadcasted_iota(jnp.int32, (CLIQUES, CLIQUES), 0)
        chosen = (clique == targets[...]).astype(jnp.float32)
        for row in range(SUB):
            measured_to_leaf[:, row, :] = jnp.dot(
                chosen, relay_measured[:, row, :],
                precision=lax.Precision.HIGHEST, preferred_element_type=jnp.float32,
            )

        def give(leaf):
            child = LEVEL2 + leaf

            @pl.when(child != me)
            def _():
                send(measured_to_leaf.at[child], whole_measured.at[quarter, relay_slot], sem_given, (child, quarter))

        repeat(LEAVES, give)

    @pl.when(jnp.logical_and(is_relay, is_second))
    def _():
        relay_tables[me - LEVEL1] = sub_tables[relay_slot]
        await_bytes(relay_tables.at[pl.ds(0, SECOND - 1)], sem_relay, 1)

    @pl.when(jnp.logical_and(is_relay, jnp.logical_not(is_second)))
    def _():
        await_bytes(relay_tables, sem_relay, 1)

    @pl.when(is_relay)
    def _():
        place = quarter * RELAYS + relay_slot

        def give_leaf(chip, plane):
            child = 2 * chip + 2 * CHIPS * (PLANES - plane // 2) + lax.rem(plane, 2)
            leaf = jnp.maximum(child - LEVEL2, 0)

            @pl.when(child >= LEVEL2)
            def _():
                to_leaf[leaf] = relay_tables[jnp.maximum(parents[child] - LEVEL1, 0), kinds[child]]
                for step in far_first[:-1]:
                    send(to_leaf.at[leaf], from_relay.at[place], sem_leaf, (child, peer(step)))

                @pl.when(child != me)
                def _():
                    send(to_leaf.at[leaf], from_relay.at[place], sem_leaf, (child, quarter))

        for chip in SERVE:
            repeat(PLANES * 2, functools.partial(give_leaf, chip))

    is_both = jnp.logical_and(is_relay, is_leaf)
    is_plain_leaf = jnp.logical_and(is_leaf, jnp.logical_not(is_relay))

    @pl.when(is_both)
    def _():
        whole_measured[quarter, relay_slot] = measured_to_leaf[me]
        from_relay[quarter * RELAYS + relay_slot] = to_leaf[me - LEVEL2]
        await_bytes(whole_measured.at[0, pl.ds(0, RELAYS - 1)], sem_given, 1)

    @pl.when(is_plain_leaf)
    def _():
        await_bytes(whole_measured.at[0], sem_given, 1)

    await_bytes(whole_l0.at[pl.ds(0, QUARTERS - 1)], sem_whole, 1)

    @pl.when(is_inner)
    def _():
        out[:, 0] = whole_l0[...] + message[...]
        out[:, 1] = jnp.zeros((QUARTERS, ROWS, K), jnp.float32)

    @pl.when(is_leaf)
    def _():
        for step in range(1, QUARTERS):
            send(whole_measured.at[quarter], whole_measured.at[quarter], sem_gather, (me, peer(step)))
        await_bytes(whole_measured.at[pl.ds(0, QUARTERS - 1)], sem_gather, 1)
        for other in range(QUARTERS):
            for relay in range(RELAYS):
                out[other, 1, relay * SUB:(relay + 1) * SUB, :] = whole_measured[other, relay]

    @pl.when(is_both)
    def _():
        await_bytes(from_relay.at[pl.ds(0, CLIQUES - 1)], sem_leaf, 1)

    @pl.when(is_plain_leaf)
    def _():
        await_bytes(from_relay, sem_leaf, 1)

    @pl.when(is_leaf)
    def _():
        for other in range(QUARTERS):
            for relay in range(RELAYS):
                rows = slice(relay * SUB, (relay + 1) * SUB)
                out[other, 0, rows, :] = whole_l0[other, rows, :] + from_relay[other * RELAYS + relay]

    await_bytes(partial_in, sem_l0, 0)
    await_bytes(whole_l0.at[pl.ds(0, QUARTERS - 1)], sem_whole, 0)

    @pl.when(is_root)
    def _():
        await_bytes(sub_measured, sem_forward, 0)
        for _ in range(QUARTERS):
            await_bytes(to_first, sem_first, 0)

    @pl.when(is_first)
    def _():
        await_bytes(to_second, sem_second, 0)

    @pl.when(me == 1)
    def _():
        await_bytes(forwarded.at[pl.ds(0, RELAYS - 1)], sem_measured, 0)

    @pl.when(is_second)
    def _():
        await_bytes(message.at[pl.ds(0, QUARTERS - 1)], sem_rows, 0)

    @pl.when(jnp.logical_and(is_second, is_relay))
    def _():
        await_bytes(sub_tables.at[pl.ds(0, RELAYS - 1)], sem_relay, 0)

    @pl.when(jnp.logical_and(is_second, jnp.logical_not(is_relay)))
    def _():
        await_bytes(sub_tables, sem_relay, 0)

    @pl.when(is_relay)
    def _():
        await_bytes(sub_measured.at[pl.ds(0, RELAYS - 1)], sem_measured, 0)
        for _ in range(QUARTERS - 1):
            await_bytes(to_leaf, sem_leaf, 0)

    @pl.when(is_both)
    def _():
        await_bytes(measured_to_leaf.at[pl.ds(0, LEAVES - 1)], sem_given, 0)
        await_bytes(to_leaf.at[pl.ds(0, LEAVES - 1)], sem_leaf, 0)

    @pl.when(jnp.logical_and(is_relay, is_inner))
    def _():
        await_bytes(measured_to_leaf.at[pl.ds(0, LEAVES)], sem_given, 0)
        await_bytes(to_leaf, sem_leaf, 0)

    @pl.when(is_leaf)
    def _():
        await_bytes(whole_measured.at[pl.ds(0, QUARTERS - 1)], sem_gather, 0)

    @pl.when(jnp.logical_not(jnp.logical_or(is_root, is_relay)))
    def _():
        await_bytes(sub_measured, sem_measured, 0)


def sweep(parents, kinds, targets, pot, measured):
    hbm, vmem = pl.BlockSpec(memory_space=pltpu.HBM), pl.BlockSpec(memory_space=pltpu.VMEM)
    f32 = jnp.float32
    scratch = [
        (ROWS, K),
        (K, K), (QUARTERS - 1, ROWS, K), (ROWS, K), (QUARTERS, ROWS, K), (QUARTERS, ROWS, K), (K, K), (ROWS, K, K),
        (3, ROWS, K),
        (FIRST, ROWS, K), (SECOND, ROWS, K), (FIRST, ROWS, K), (RELAYS, 3, SUB, K), (SECOND, 3, SUB, K),
        (RELAYS, SUB, K), (RELAYS, SUB, K), (CLIQUES, SUB, K), (CLIQUES, SUB, K), (QUARTERS, RELAYS, SUB, K),
        (LEAVES, SUB, K), (QUARTERS * RELAYS, SUB, K),
    ]
    return pl.pallas_call(
        sweep_kernel,
        out_shape=(
            jax.ShapeDtypeStruct((QUARTERS, 2, ROWS, K), f32),
            jax.ShapeDtypeStruct((ROWS, K, K), f32),
        ),
        in_specs=[hbm] * 5,
        out_specs=(vmem, vmem),
        scratch_shapes=[
            pltpu.SMEM((CLIQUES,), jnp.int32), pltpu.SMEM((CLIQUES,), jnp.int32), pltpu.VMEM((1, CLIQUES), jnp.int32),
            *(pltpu.VMEM(shape, f32) for shape in scratch),
            pltpu.SemaphoreType.DMA((4,)), pltpu.SemaphoreType.DMA((QUARTERS,)),
            *[pltpu.SemaphoreType.DMA((2,))] * 11,
            pltpu.SemaphoreType.REGULAR, pltpu.SemaphoreType.REGULAR,
        ],
        compiler_params=pltpu.CompilerParams(
            collective_id=0, has_side_effects=True, vmem_limit_bytes=16 * 1024 * 1024
        ),
        name="sweep",
    )(parents, kinds, targets, pot, measured)


BLOCK = 8


def finish_kernel(final, pot, marginal_hbm, updated_hbm, marginal, updated, sem):
    me = lax.axis_index("wide")
    quarter = lax.axis_index("narrow")
    cells = final[:, 0]
    largest = jnp.max(cells)
    weights = jnp.exp(cells - largest)
    scale = jnp.float32(K * K) / jnp.sum(weights)
    whole = weights * scale
    marginal[...] = jnp.exp(final[quarter, 0] - largest) * scale
    copies = [pltpu.make_async_copy(marginal, marginal_hbm, sem.at[0])]
    copies[0].start()
    term = jnp.where(me >= LEVEL2, jnp.float32(0.5) * (whole - final[:, 1]), jnp.float32(0.0)).reshape(K, K)
    for block in range(ROWS // BLOCK):
        rows = slice(block * BLOCK, (block + 1) * BLOCK)
        updated[rows] = pot[rows] - term[None]
        copies.append(pltpu.make_async_copy(updated.at[rows], updated_hbm.at[rows], sem.at[1 + block]))
        copies[-1].start()
    for copy in copies:
        copy.wait()


def finish(final, pot):
    hbm, vmem = pl.BlockSpec(memory_space=pltpu.HBM), pl.BlockSpec(memory_space=pltpu.VMEM)
    shapes = (ROWS, K), (ROWS, K, K)
    return pl.pallas_call(
        finish_kernel,
        out_shape=tuple(jax.ShapeDtypeStruct(shape, jnp.float32) for shape in shapes),
        in_specs=[vmem, vmem],
        out_specs=(hbm, hbm),
        scratch_shapes=[*(pltpu.VMEM(shape, jnp.float32) for shape in shapes), pltpu.SemaphoreType.DMA((1 + ROWS // BLOCK,))],
        compiler_params=pltpu.CompilerParams(vmem_limit_bytes=16 * 1024 * 1024),
        name="finish",
    )(final, pot)


def body(potentials, parents, separator_excluded, measurement_clique, measured):
    parents, separator_excluded, measurement_clique, measured, potentials = (
        pltpu.with_memory_space_constraint(array, pltpu.HBM)
        for array in (parents, separator_excluded, measurement_clique[None], measured[0], potentials[0])
    )
    pot = potentials
    final, pot = sweep(parents, separator_excluded, measurement_clique, pot, measured)
    marginal, updated = finish(final, pot)
    return marginal[None], updated[None]


def solution(mesh):
    return jax.shard_map(
        body,
        mesh=mesh,
        in_specs=(P("wide", "narrow", None, None), P(), P(), P(), P("wide", "narrow", None)),
        out_specs=(P("wide", "narrow", None), P("wide", "narrow", None, None)),
        check_vma=False,
    )
```

```python
import functools

import jax
import jax.numpy as jnp
from jax import lax
from jax.experimental import pallas as pl
from jax.experimental.pallas import tpu as pltpu
from jax.sharding import PartitionSpec as P

MESH = pl.DeviceIdType.MESH
K = 128
QUARTERS = 4
ROWS = K // QUARTERS
CLIQUES = 64
LEVEL1, LEVEL2 = 5, 21
FIRST = LEVEL1 - 1
SECOND = LEVEL2 - LEVEL1
LEAVES = CLIQUES - LEVEL2
RELAYS = 16
SUB = ROWS // RELAYS
CHIPS, PLANES = 8, 3


FARTHEST = (5, 7, 6, 8, 11, 3, 9, 12, 4, 10, 13, 1, 14, 2, 15, 0)


SERVE = (0, 1, 2, 3, 6, 5, 4, 7)


def sweep_kernel(
    parents_hbm, kinds_hbm, targets_hbm, pot_hbm, measured_hbm, out, pot,
    parents, kinds, targets, measured,
    partial, partial_in, own_l0, whole_l0, message, message_t, pot_t, tables,
    to_first, to_second, candidates, sub_tables, relay_tables,
    sub_measured, forwarded, relay_measured, measured_to_leaf, whole_measured, to_leaf, from_relay,
    sem_small, sem_pot,
    sem_l0, sem_whole, sem_first, sem_second, sem_rows, sem_relay, sem_forward, sem_measured, sem_given, sem_gather, sem_leaf,
    sem_near, sem_far,
):
    me = lax.axis_index("wide")
    quarter = lax.axis_index("narrow")
    is_root = me == 0
    is_first = jnp.logical_and(me >= 1, me < LEVEL1)
    is_second = jnp.logical_and(me >= LEVEL1, me < LEVEL2)
    is_leaf = me >= LEVEL2
    is_inner = me < LEVEL2
    odd = lax.rem(me, 2)
    is_relay = jnp.logical_and(odd == 1, lax.rem(me, 2 * CHIPS) < CHIPS)
    is_early = me < LEVEL1
    peers = QUARTERS - 1

    def peer(step):
        return lax.rem(quarter + step, QUARTERS)

    def relay_device(relay):
        return 2 * CHIPS * (relay // (CHIPS // 2)) + 2 * lax.rem(relay, CHIPS // 2) + 1

    def rows_of(part):
        return pl.ds(pl.multiple_of(part * ROWS, ROWS), ROWS)

    def repeat(count, function, unroll=1):
        def run(index, carry):
            function(index)
            return carry

        lax.fori_loop(0, count, run, 0, unroll=unroll)

    def send(source, target, sem, device):
        pltpu.make_async_remote_copy(
            src_ref=source, dst_ref=target, send_sem=sem.at[0], recv_sem=sem.at[1],
            device_id=device, device_id_type=MESH,
        ).start()

    def await_bytes(like, sem, which):
        pltpu.make_async_copy(like, like, sem.at[which]).wait()

    small = [
        pltpu.make_async_copy(source, target, sem_small.at[index])
        for index, (source, target) in enumerate(
            ((parents_hbm, parents), (kinds_hbm, kinds), (targets_hbm, targets), (measured_hbm, measured))
        )
    ]

    def pot_copy(step):
        rows = rows_of(peer(step))
        return pltpu.make_async_copy(pot_hbm.at[:, rows], pot.at[:, rows], sem_pot.at[step])

    far_first = (2, 1, 3, 0)
    order = far_first
    for step in order:
        pot_copy(step).start()
    for copy in small:
        copy.start()

    barrier = pltpu.get_barrier_semaphore()

    def greet(wide, narrow):
        pl.semaphore_signal(barrier, inc=1, device_id=(wide, narrow), device_id_type=MESH)

    for step in range(1, QUARTERS):
        greet(me, peer(step))

    @pl.when(is_root)
    def _():
        for child in range(1, LEVEL1):
            greet(child, quarter)

    @pl.when(is_first)
    def _():
        for step in range(FIRST - 1):
            greet(1 + lax.rem(me + step, FIRST), quarter)
        repeat(CLIQUES - LEVEL1, lambda index: greet(LEVEL1 + index, quarter))

    @pl.when(jnp.logical_and(jnp.logical_not(is_early), is_relay))
    def _():
        def one(index):
            greet(LEVEL1 + index + (index >= me - LEVEL1).astype(jnp.int32), quarter)

        repeat(CLIQUES - LEVEL1 - 1, one)

    def partial_lse(step):
        base = peer(step) * ROWS

        def one(block):
            rows = pl.ds(pl.multiple_of(base + block * 8, 8), 8)
            slab = pot[:, rows, :]
            largest = jnp.max(slab, axis=0)
            partial[rows, :] = largest + jnp.log(jnp.sum(jnp.exp(slab - largest[None]), axis=0))

        pot_copy(step).wait()
        repeat(ROWS // 8, one, unroll=4)

    partial_lse(order[0])

    @pl.when(is_root)
    def _():
        pl.semaphore_wait(barrier, peers)

    @pl.when(is_first)
    def _():
        pl.semaphore_wait(barrier, peers + FIRST)
        pl.semaphore_signal(sem_near, inc=1, device_id=(0, quarter), device_id_type=MESH)

    @pl.when(jnp.logical_not(is_early))
    def _():
        pl.semaphore_wait(barrier, peers + RELAYS - is_relay.astype(jnp.int32) + 2)

    @pl.when(jnp.logical_or(is_second, jnp.logical_and(is_relay, is_leaf)))
    def _():
        for child in range(1, LEVEL1):
            pl.semaphore_signal(sem_far, inc=1, device_id=(child, quarter), device_id_type=MESH)

    for step in order:
        if step != order[0]:
            partial_lse(step)
        if step:
            send(partial.at[rows_of(peer(step))], partial_in.at[step - 1], sem_l0, (me, peer(step)))

    for copy in small:
        copy.wait()
    for relay in range(RELAYS):
        sub_measured[relay] = measured[relay * SUB:(relay + 1) * SUB, :]

    def give_measured(relay):
        @pl.when(me != relay_device(relay))
        def _():
            send(sub_measured.at[relay], relay_measured.at[me], sem_measured, (relay_device(relay), quarter))

    @pl.when(jnp.logical_not(is_early))
    def _():
        repeat(RELAYS, give_measured)

    @pl.when(is_inner)
    def _():
        def turn(a0):
            pot_t[a0] = pot[a0].T

        repeat(ROWS, turn, unroll=4)

    def gather_l0():
        await_bytes(partial_in, sem_l0, 1)
        mine = partial[rows_of(quarter), :]
        largest = jnp.maximum(mine, jnp.max(partial_in[...], axis=0))
        summed = jnp.exp(mine - largest) + jnp.sum(jnp.exp(partial_in[...] - largest[None]), axis=0)
        own_l0[...] = largest + jnp.log(summed)

    def share_l0():
        for step in range(1, QUARTERS):
            send(own_l0, whole_l0.at[quarter], sem_whole, (me, peer(step)))
        whole_l0[quarter] = own_l0[...]

    @pl.when(is_root)
    def _():
        message[...] = jnp.zeros_like(message)

    @pl.when(jnp.logical_not(is_root))
    def _():
        gather_l0()
        share_l0()

    @pl.when(is_first)
    def _():
        await_bytes(message, sem_first, 1)

    @pl.when(is_second)
    def _():
        await_bytes(candidates, sem_second, 1)
        message[quarter] = candidates[jnp.maximum(parents[me] - 1, 0)]
        for step in far_first[:-1]:
            send(message.at[quarter], message.at[quarter], sem_rows, (me, peer(step)))
        await_bytes(message.at[pl.ds(0, QUARTERS - 1)], sem_rows, 1)

    @pl.when(is_inner)
    def _():
        for other in range(QUARTERS):
            message_t[:, other * ROWS:(other + 1) * ROWS] = message[other].T

        def eight(group):
            rows = pl.ds(pl.multiple_of(group * 8, 8), 8)
            for kind in (1, 2):
                tops, totals = [], []
                for step in range(8):
                    a0 = group * 8 + step
                    if kind == 1:
                        belief = (pot[a0].reshape(QUARTERS, ROWS, K) + message[...]).reshape(K, K)
                    else:
                        belief = pot_t[a0] + message_t[...]
                    largest = jnp.max(belief, axis=0, keepdims=True)
                    tops.append(largest)
                    totals.append(jnp.sum(jnp.exp(belief - largest), axis=0, keepdims=True))
                tables[kind, rows, :] = jnp.concatenate(tops, 0) + jnp.log(jnp.concatenate(totals, 0))

        repeat(ROWS // 8, eight, unroll=2)

    @pl.when(is_root)
    def _():
        gather_l0()

    @pl.when(is_inner)
    def _():
        tables[0] = own_l0[...] + message[quarter]

    @pl.when(is_root)
    def _():
        pl.semaphore_wait(sem_near, FIRST)
        for child in reversed(range(FIRST)):
            to_first[child] = tables[kinds[1 + child]]
            for step in far_first:
                send(to_first.at[child], message.at[quarter], sem_first, (1 + child, peer(step)))
        send(sub_measured, forwarded, sem_forward, (1, quarter))

    @pl.when(is_first)
    def _():
        pl.semaphore_wait(sem_far, SECOND + 10)

        for child in FARTHEST:
            to_second[child] = tables[kinds[LEVEL1 + child]]
            send(to_second.at[child], candidates.at[me - 1], sem_second, (LEVEL1 + child, quarter))

        repeat(RELAYS, give_measured)

    @pl.when(me == 1)
    def _():
        await_bytes(forwarded, sem_forward, 1)

        def give(index):
            relay = 1 + index
            send(forwarded.at[relay], relay_measured.at[0], sem_measured, (relay_device(relay), quarter))

        repeat(RELAYS - 1, give)
        relay_measured[0] = forwarded[0]

    @pl.when(is_second)
    def _():
        slot = me - LEVEL1
        for kind in range(3):
            for relay in range(RELAYS):
                sub_tables[relay, kind] = tables[kind, relay * SUB:(relay + 1) * SUB, :]

        def give_tables(relay):
            @pl.when(me != relay_device(relay))
            def _():
                send(sub_tables.at[relay], relay_tables.at[slot], sem_relay, (relay_device(relay), quarter))

        repeat(RELAYS, give_tables)

    @pl.when(is_root)
    def _():
        share_l0()

    relay_slot = (CHIPS // 2) * (me // (2 * CHIPS)) + lax.rem(me, 2 * CHIPS) // 2

    @pl.when(me == 1)
    def _():
        await_bytes(relay_measured.at[pl.ds(0, CLIQUES - 2)], sem_measured, 1)

    @pl.when(jnp.logical_and(is_relay, me != 1))
    def _():
        await_bytes(relay_measured.at[pl.ds(0, CLIQUES - 1)], sem_measured, 1)

    @pl.when(is_relay)
    def _():
        relay_measured[me] = sub_measured[relay_slot]
        clique = lax.broadcasted_iota(jnp.int32, (CLIQUES, CLIQUES), 0)
        chosen = (clique == targets[...]).astype(jnp.float32)
        for row in range(SUB):
            measured_to_leaf[:, row, :] = jnp.dot(
                chosen, relay_measured[:, row, :],
                precision=lax.Precision.HIGHEST, preferred_element_type=jnp.float32,
            )

        def give(leaf):
            child = LEVEL2 + leaf

            @pl.when(child != me)
            def _():
                send(measured_to_leaf.at[child], whole_measured.at[quarter, relay_slot], sem_given, (child, quarter))

        repeat(LEAVES, give)

    @pl.when(jnp.logical_and(is_relay, is_second))
    def _():
        relay_tables[me - LEVEL1] = sub_tables[relay_slot]
        await_bytes(relay_tables.at[pl.ds(0, SECOND - 1)], sem_relay, 1)

    @pl.when(jnp.logical_and(is_relay, jnp.logical_not(is_second)))
    def _():
        await_bytes(relay_tables, sem_relay, 1)

    @pl.when(is_relay)
    def _():
        place = quarter * RELAYS + relay_slot

        def give_leaf(chip, plane):
            child = 2 * chip + 2 * CHIPS * (PLANES - plane // 2) + lax.rem(plane, 2)
            leaf = jnp.maximum(child - LEVEL2, 0)

            @pl.when(child >= LEVEL2)
            def _():
                to_leaf[leaf] = relay_tables[jnp.maximum(parents[child] - LEVEL1, 0), kinds[child]]
                for step in far_first[:-1]:
                    send(to_leaf.at[leaf], from_relay.at[place], sem_leaf, (child, peer(step)))

                @pl.when(child != me)
                def _():
                    send(to_leaf.at[leaf], from_relay.at[place], sem_leaf, (child, quarter))

        for chip in SERVE:
            repeat(PLANES * 2, functools.partial(give_leaf, chip))

    is_both = jnp.logical_and(is_relay, is_leaf)
    is_plain_leaf = jnp.logical_and(is_leaf, jnp.logical_not(is_relay))

    @pl.when(is_both)
    def _():
        whole_measured[quarter, relay_slot] = measured_to_leaf[me]
        from_relay[quarter * RELAYS + relay_slot] = to_leaf[me - LEVEL2]
        await_bytes(whole_measured.at[0, pl.ds(0, RELAYS - 1)], sem_given, 1)

    @pl.when(is_plain_leaf)
    def _():
        await_bytes(whole_measured.at[0], sem_given, 1)

    await_bytes(whole_l0.at[pl.ds(0, QUARTERS - 1)], sem_whole, 1)

    @pl.when(is_inner)
    def _():
        out[:, 0] = whole_l0[...] + message[...]
        out[:, 1] = jnp.zeros((QUARTERS, ROWS, K), jnp.float32)

    @pl.when(is_leaf)
    def _():
        for step in range(1, QUARTERS):
            send(whole_measured.at[quarter], whole_measured.at[quarter], sem_gather, (me, peer(step)))
        await_bytes(whole_measured.at[pl.ds(0, QUARTERS - 1)], sem_gather, 1)
        for other in range(QUARTERS):
            for relay in range(RELAYS):
                out[other, 1, relay * SUB:(relay + 1) * SUB, :] = whole_measured[other, relay]

    @pl.when(is_both)
    def _():
        await_bytes(from_relay.at[pl.ds(0, CLIQUES - 1)], sem_leaf, 1)

    @pl.when(is_plain_leaf)
    def _():
        await_bytes(from_relay, sem_leaf, 1)

    @pl.when(is_leaf)
    def _():
        for other in range(QUARTERS):
            for relay in range(RELAYS):
                rows = slice(relay * SUB, (relay + 1) * SUB)
                out[other, 0, rows, :] = whole_l0[other, rows, :] + from_relay[other * RELAYS + relay]

    await_bytes(partial_in, sem_l0, 0)
    await_bytes(whole_l0.at[pl.ds(0, QUARTERS - 1)], sem_whole, 0)

    @pl.when(is_root)
    def _():
        await_bytes(sub_measured, sem_forward, 0)
        for _ in range(QUARTERS):
            await_bytes(to_first, sem_first, 0)

    @pl.when(is_first)
    def _():
        await_bytes(to_second, sem_second, 0)

    @pl.when(me == 1)
    def _():
        await_bytes(forwarded.at[pl.ds(0, RELAYS - 1)], sem_measured, 0)

    @pl.when(is_second)
    def _():
        await_bytes(message.at[pl.ds(0, QUARTERS - 1)], sem_rows, 0)

    @pl.when(jnp.logical_and(is_second, is_relay))
    def _():
        await_bytes(sub_tables.at[pl.ds(0, RELAYS - 1)], sem_relay, 0)

    @pl.when(jnp.logical_and(is_second, jnp.logical_not(is_relay)))
    def _():
        await_bytes(sub_tables, sem_relay, 0)

    @pl.when(is_relay)
    def _():
        await_bytes(sub_measured.at[pl.ds(0, RELAYS - 1)], sem_measured, 0)
        for _ in range(QUARTERS - 1):
            await_bytes(to_leaf, sem_leaf, 0)

    @pl.when(is_both)
    def _():
        await_bytes(measured_to_leaf.at[pl.ds(0, LEAVES - 1)], sem_given, 0)
        await_bytes(to_leaf.at[pl.ds(0, LEAVES - 1)], sem_leaf, 0)

    @pl.when(jnp.logical_and(is_relay, is_inner))
    def _():
        await_bytes(measured_to_leaf.at[pl.ds(0, LEAVES)], sem_given, 0)
        await_bytes(to_leaf, sem_leaf, 0)

    @pl.when(is_leaf)
    def _():
        await_bytes(whole_measured.at[pl.ds(0, QUARTERS - 1)], sem_gather, 0)

    @pl.when(jnp.logical_not(jnp.logical_or(is_root, is_relay)))
    def _():
        await_bytes(sub_measured, sem_measured, 0)


def sweep(parents, kinds, targets, pot, measured):
    hbm, vmem = pl.BlockSpec(memory_space=pltpu.HBM), pl.BlockSpec(memory_space=pltpu.VMEM)
    f32 = jnp.float32
    scratch = [
        (ROWS, K),
        (K, K), (QUARTERS - 1, ROWS, K), (ROWS, K), (QUARTERS, ROWS, K), (QUARTERS, ROWS, K), (K, K), (ROWS, K, K),
        (3, ROWS, K),
        (FIRST, ROWS, K), (SECOND, ROWS, K), (FIRST, ROWS, K), (RELAYS, 3, SUB, K), (SECOND, 3, SUB, K),
        (RELAYS, SUB, K), (RELAYS, SUB, K), (CLIQUES, SUB, K), (CLIQUES, SUB, K), (QUARTERS, RELAYS, SUB, K),
        (LEAVES, SUB, K), (QUARTERS * RELAYS, SUB, K),
    ]
    return pl.pallas_call(
        sweep_kernel,
        out_shape=(
            jax.ShapeDtypeStruct((QUARTERS, 2, ROWS, K), f32),
            jax.ShapeDtypeStruct((ROWS, K, K), f32),
        ),
        in_specs=[hbm] * 5,
        out_specs=(vmem, vmem),
        scratch_shapes=[
            pltpu.SMEM((CLIQUES,), jnp.int32), pltpu.SMEM((CLIQUES,), jnp.int32), pltpu.VMEM((1, CLIQUES), jnp.int32),
            *(pltpu.VMEM(shape, f32) for shape in scratch),
            pltpu.SemaphoreType.DMA((4,)), pltpu.SemaphoreType.DMA((QUARTERS,)),
            *[pltpu.SemaphoreType.DMA((2,))] * 11,
            pltpu.SemaphoreType.REGULAR, pltpu.SemaphoreType.REGULAR,
        ],
        compiler_params=pltpu.CompilerParams(
            collective_id=0, has_side_effects=True, vmem_limit_bytes=16 * 1024 * 1024
        ),
        name="sweep",
    )(parents, kinds, targets, pot, measured)


BLOCK = 8


def finish_kernel(final, pot, marginal_hbm, updated_hbm, marginal, updated, sem):
    me = lax.axis_index("wide")
    quarter = lax.axis_index("narrow")
    cells = final[:, 0]
    largest = jnp.max(cells, axis=(0, 1, 2), keepdims=True)
    weights = jnp.exp(cells - largest)
    scale = jnp.float32(K * K) / jnp.sum(weights, axis=(0, 1, 2), keepdims=True)
    whole = weights * scale
    marginal[...] = jnp.exp(final[quarter, 0] - largest[0]) * scale[0]
    copies = [pltpu.make_async_copy(marginal, marginal_hbm, sem.at[0])]
    copies[0].start()
    term = jnp.where(me >= LEVEL2, jnp.float32(0.5) * (whole - final[:, 1]), jnp.float32(0.0)).reshape(K, K)
    for block in range(ROWS // BLOCK):
        rows = slice(block * BLOCK, (block + 1) * BLOCK)
        updated[rows] = pot[rows] - term[None]
        copies.append(pltpu.make_async_copy(updated.at[rows], updated_hbm.at[rows], sem.at[1 + block]))
        copies[-1].start()
    for copy in copies:
        copy.wait()


def finish(final, pot):
    hbm, vmem = pl.BlockSpec(memory_space=pltpu.HBM), pl.BlockSpec(memory_space=pltpu.VMEM)
    shapes = (ROWS, K), (ROWS, K, K)
    return pl.pallas_call(
        finish_kernel,
        out_shape=tuple(jax.ShapeDtypeStruct(shape, jnp.float32) for shape in shapes),
        in_specs=[vmem, vmem],
        out_specs=(hbm, hbm),
        scratch_shapes=[*(pltpu.VMEM(shape, jnp.float32) for shape in shapes), pltpu.SemaphoreType.DMA((1 + ROWS // BLOCK,))],
        compiler_params=pltpu.CompilerParams(vmem_limit_bytes=16 * 1024 * 1024),
        name="finish",
    )(final, pot)


def body(potentials, parents, separator_excluded, measurement_clique, measured):
    parents, separator_excluded, measurement_clique, measured, potentials = (
        pltpu.with_memory_space_constraint(array, pltpu.HBM)
        for array in (parents, separator_excluded, measurement_clique[None], measured[0], potentials[0])
    )
    pot = potentials
    final, pot = sweep(parents, separator_excluded, measurement_clique, pot, measured)
    marginal, updated = finish(final, pot)
    return marginal[None], updated[None]


def solution(mesh):
    return jax.shard_map(
        body,
        mesh=mesh,
        in_specs=(P("wide", "narrow", None, None), P(), P(), P(), P("wide", "narrow", None)),
        out_specs=(P("wide", "narrow", None), P("wide", "narrow", None, None)),
        check_vma=False,
    )
```
